256 devices in a mesh: rep: 16 (over y_lo, z), slab: 16 (over y_hi, x, core).
Axes of the slice: x: 4, y: 4 (y_hi: 2, y_lo: 2; y = y_hi * 2 + y_lo), z: 8, core: 2. Of those that a mesh axis runs over, the one named last changes fastest.
Arguments:
- positions: float32 [16, 3, 98304], P('rep', None, 'slab'), as said below
- velocities: float32 [16, 3, 98304], P('rep', None, 'slab'), may hold values from -6 to 6
- strength: float32 [98304], P('slab'), may hold values from 0.5 to 2
- inv_mass: float32 [98304], P('slab'), may hold values from 0.25 to 1
- solute: int32 [98304], P('slab'), may hold values 0 or 1
- scales: float32 [16], P('rep'), may hold values from 0.3 to 1
- neighbours: int32 [768, 4], P('slab'), may hold values from 0 to 767, as said below
- counts: int32 [768], P('slab'), may hold values from 1 to 4
- partner: int32 [16], P('rep'), may hold values from 0 to 15, as said below
- accept: int32 [16], P('rep'), may hold values from 0 to 1, as said below
Outputs:
- new_positions: float32 [16, 3, 98304], P('rep', None, 'slab')
- new_velocities: float32 [16, 3, 98304], P('rep', None, 'slab')
- exponent: float32 [16], P('rep')
The draws below stay inside these ranges and needn't reach their ends.
Inputs may be any that keep to these rules, and one draw needn't show every extreme that they name: `positions`: the x component of an atom of slab t (atoms t * 48 * 128 onward) lies in [t, t + 1); the others in [0, 2). `neighbours`: each listed block lies in the block's own slab, among the last 16 blocks of the previous slab, or among the first 16 blocks of the next slab, slabs taken periodically; every block lists itself first. Replicas are matched in pairs of neighbouring indices r and r + 1, all starting on the same parity; a replica left out is its own partner. `accept`: equal for both members of a pair; 0 for a replica that is its own partner.
All inputs are finite; a program needn't handle non-finite values. No bound on the sum of `solute` on one device may be relied on, other than what follows from the above.
Results may differ from the reference program's by a relative error of at most 0.0003.
Values sent between devices are 32-bit elements; how exact they have to be, the bound alone decides.
A program may use at most 64 MiB of HBM per device.

```python
import math
import jax
import jax.numpy as jnp
from jax import lax

BLK_DEV = 48
NB = 4
RIM = 16
REPLICAS = 16
BLOCKS = 768
ATOMS = 98304
N_SLAB = 16


def pairing(key):
    first, second = jax.random.split(key)
    phase = jax.random.randint(first, (), 0, 2)
    replica = jnp.arange(REPLICAS, dtype=jnp.int32)
    upward = (replica - phase) % 2 == 0
    mate = jnp.where(upward, replica + 1, replica - 1)
    mate = jnp.where((mate < 0) | (mate >= REPLICAS), replica, mate).astype(jnp.int32)
    lowest = jnp.minimum(replica, mate)
    coins = jax.random.randint(second, (REPLICAS,), 0, 2)
    coin = coins[lowest]
    coin = jnp.where(lowest == phase, 1, jnp.where(lowest == phase + 2, 0, coin))
    taken = jnp.where(mate == replica, 0, coin).astype(jnp.int32)
    return (mate, taken)


def draw_partner(key, part):
    mate, taken = pairing(key)
    return mate


def draw_accept(key, part):
    mate, taken = pairing(key)
    return taken


def draw_positions(key, part):
    key = jax.random.fold_in(key, 11)
    first, second = jax.random.split(key)
    along = jax.random.uniform(first, (REPLICAS, 1, ATOMS), jnp.float32)
    owner = (jnp.arange(ATOMS) // (BLK_DEV * 128)).astype(jnp.float32)
    across = jax.random.uniform(second, (REPLICAS, 2, ATOMS), jnp.float32) * 2.0
    return jnp.concatenate([owner[None, None, :] + along * 0.999, across], axis=1)


def draw_neighbours(key, part):
    key = jax.random.fold_in(key, 12)
    first, second, third = jax.random.split(key, 3)
    block = jnp.arange(BLOCKS, dtype=jnp.int32)[:, None]
    owner = block // BLK_DEV
    local = block % BLK_DEV
    side = jax.random.randint(first, (BLOCKS, NB), 0, 3)
    inner = jax.random.randint(second, (BLOCKS, NB), 0, BLK_DEV)
    edge = jax.random.randint(third, (BLOCKS, NB), 0, RIM)
    lower = (owner - 1) % N_SLAB * BLK_DEV
    upper = (owner + 1) % N_SLAB * BLK_DEV
    pick = jnp.where(side == 0, owner * BLK_DEV + inner, jnp.where(side == 1, lower + BLK_DEV - 1 - edge, upper + edge))
    column = jnp.arange(NB, dtype=jnp.int32)[None, :]
    pick = jnp.where(column == 0, block, pick)
    leading = local == 0
    pick = jnp.where(leading & (column == 1), lower + BLK_DEV - RIM, pick)
    pick = jnp.where(leading & (column == 2), upper + RIM - 1, pick)
    return pick.astype(jnp.int32)


def draw_counts(key, part):
    key = jax.random.fold_in(key, 13)
    number = jax.random.randint(key, (BLOCKS,), 1, NB + 1)
    local = jnp.arange(BLOCKS, dtype=jnp.int32) % BLK_DEV
    return jnp.where(local == 0, NB, number).astype(jnp.int32)


def place_ends(result, key, low, largest):
    longest = result.shape.index(max(result.shape))
    spots = []
    for shift in (0, 1):
        where = [jax.random.randint(jax.random.fold_in(key, axis), (), 0, length) for axis, length in enumerate(result.shape)]
        where[longest] = (where[longest] + shift) % result.shape[longest]
        spots.append(tuple(where))
    return result.at[spots[0]].set(low).at[spots[1]].set(largest)


def block_levels(key, shape, cuts, smallest, high):
    def one(dim, shards_of):
        heights = jax.random.uniform(jax.random.fold_in(jax.random.fold_in(key, 6), dim), (shards_of,), jnp.float32, smallest / len(cuts), high / len(cuts))
        return jnp.repeat(jnp.exp(heights), shape[dim] // shards_of).reshape((-1,) + (1,) * (len(shape) - dim - 1))

    loudness = one(*cuts[0])
    for cut in cuts[1:]:
        loudness = loudness * one(*cut)
    return loudness


def bell_draw(rng, shape, deviation, limit, shards=(), held_as=jnp.bfloat16):
    result = jax.random.normal(rng, shape, jnp.float32) * deviation
    if len(shards) > 0:
        result = block_levels(rng, shape, shards, -0.22, 0.18) * result
    return jnp.clip(result, min=-limit, max=limit).astype(held_as)


def setup_inputs(seed: int = 0) -> dict:
    key_list = jax.random.split(jax.random.key(seed), 11)
    positions = draw_positions(jax.random.fold_in(key_list[10], 71), 0)
    velocities = bell_draw(key_list[1], (REPLICAS, 3, ATOMS), 1.0, 6.0, ((0, 16), (2, 16)), jnp.float32)
    strength = jnp.clip(jnp.exp(math.log(2.0) - 1.3862944 * jax.random.uniform(key_list[2], (ATOMS,), jnp.float32) ** block_levels(key_list[2], (ATOMS,), ((0, 16),), -0.2, 0.2)), 0.5, 2.0)
    inv_mass = jnp.clip(jnp.exp(math.log(1.0) - 1.3862944 * jax.random.uniform(key_list[3], (ATOMS,), jnp.float32) ** block_levels(key_list[3], (ATOMS,), ((0, 16),), -0.2, 0.2)), 0.25, 1.0)
    solute = place_ends((jax.random.randint(key_list[4], (ATOMS,), 0, 4) < 1).astype(jnp.int32), jax.random.fold_in(key_list[4], 1), 0, 1)
    scales = jnp.clip(0.3 + 0.7 * jax.random.uniform(key_list[5], (REPLICAS,), jnp.float32) ** block_levels(key_list[5], (REPLICAS,), ((0, 16),), -0.2, 0.2), 0.3, 1.0)
    neighbours = draw_neighbours(jax.random.fold_in(key_list[10], 71), 0)
    counts = draw_counts(jax.random.fold_in(key_list[10], 71), 0)
    partner = draw_partner(jax.random.fold_in(key_list[10], 71), 0)
    accept = draw_accept(jax.random.fold_in(key_list[10], 71), 0)
    return {"positions": positions, "velocities": velocities, "strength": strength, "inv_mass": inv_mass, "solute": solute, "scales": scales, "neighbours": neighbours, "counts": counts, "partner": partner, "accept": accept}


SIGMA = 0.35
BOX = 2.0
STEP = 0.02
HIGH = lax.Precision.HIGHEST

def constants(periods):
    hcoef = jnp.array([p * p / (2.0 * math.pi ** 2) / (2.0 * SIGMA ** 2) for p in periods], jnp.float32).reshape(3, 1)
    shift = sum((p * p / (2.0 * math.pi ** 2) / (2.0 * SIGMA ** 2) for p in periods))
    fcoef = jnp.array([p / math.pi / (2.0 * SIGMA ** 2) for p in periods], jnp.float32).reshape(3, 1)
    factors = jnp.array([2.0 * math.pi / p for p in periods], jnp.float32).reshape(3, 1)
    return (hcoef, shift, fcoef, factors)

def angle_features(pos, factors):
    theta = pos * factors
    return (jnp.cos(theta), jnp.sin(theta))

def field_sums(ca_own, sa_own, ca_all, sa_all, cols_all, index, masks, hcoef, shift):
    own_c = (ca_own * hcoef).reshape(3, -1, 128)
    own_s = (sa_own * hcoef).reshape(3, -1, 128)
    blk_c = ca_all.reshape(3, -1, 128)
    blk_s = sa_all.reshape(3, -1, 128)
    blk_cols = cols_all.reshape(cols_all.shape[0], -1, 128)
    total = jnp.zeros((cols_all.shape[0],) + own_c.shape[1:], jnp.float32)
    for entry in range(len(masks)):
        pick = index[:, entry]
        far_c = jnp.take(blk_c, pick, axis=1)
        far_s = jnp.take(blk_s, pick, axis=1)
        far_cols = jnp.take(blk_cols, pick, axis=1)
        inner = jnp.einsum('cbi,cbj->bij', own_c, far_c, precision=HIGH) + jnp.einsum('cbi,cbj->bij', own_s, far_s, precision=HIGH)
        kernel = jnp.exp(inner - shift)
        total = total + jnp.einsum('bij,fbj->fbi', kernel, far_cols, precision=HIGH) * masks[entry][None, :, None]
    return total.reshape(cols_all.shape[0], -1)

def reference(positions, velocities, strength, inv_mass, solute, scales, neighbours, counts, partner, accept):
    periods = [float(N_SLAB), BOX, BOX]
    hcoef, shift, fcoef, factors = constants(periods)
    flags = solute.astype(jnp.float32)
    masks = [(counts > entry).astype(jnp.float32) for entry in range(NB)]

    def one_replica(state):
        pos, vel, level = state
        root = jnp.sqrt(level)
        scale = strength * jnp.where(flags > 0.5, root, jnp.float32(1.0))

        def force(x):
            ca, sa = angle_features(x, factors)
            cols = jnp.concatenate([scale * ca, scale * sa], axis=0)
            sums = field_sums(ca, sa, ca, sa, cols, neighbours, masks, hcoef, shift)
            return fcoef * scale * (sa * sums[:3] - ca * sums[3:])
        for turn in range(2):
            vel = vel + STEP * inv_mass * force(pos)
            pos = pos + STEP * vel
        ca, sa = angle_features(pos, factors)
        cols = jnp.stack([strength * flags, strength])
        sums = field_sums(ca, sa, ca, sa, cols, neighbours, masks, hcoef, shift)
        inside, every = (sums[0], sums[1])
        solute_sum = 0.5 * jnp.sum(strength * flags * inside)
        mixed_sum = 0.5 * jnp.sum(strength * (flags * (every - inside) + (1.0 - flags) * inside))
        return (pos, vel, solute_sum, mixed_sum)
    moved, speeds, solute_sums, mixed_sums = lax.map(one_replica, (positions, velocities, scales))
    other_level = scales[partner]
    exponent = ((other_level - scales) * (solute_sums - solute_sums[partner]) + (jnp.sqrt(other_level) - jnp.sqrt(scales)) * (mixed_sums - mixed_sums[partner])) / ATOMS
    taken = (accept == 1)[:, None, None]
    new_positions = jnp.where(taken, moved[partner], moved)
    new_velocities = jnp.where(taken, speeds[partner], speeds)
    return (new_positions, new_velocities, exponent)
```

```python
import functools
import math

import jax
import jax.numpy as jnp
from jax import lax
from jax.experimental import pallas as pl
from jax.experimental.pallas import tpu as pltpu
from jax.sharding import PartitionSpec as P

NB = 4
RIM = 16
SIGMA = 0.35
BOX = 2.0
STEP = 0.02
NONE = -1000.0
MESH = pl.DeviceIdType.MESH
F32 = jnp.float32
BF16 = jnp.bfloat16
SINE = (
    6.28318530717,
    -41.34170211,
    81.60522621,
    -76.70428132,
    42.00980576,
    -14.39413556,
)


def dot(a, b):
    return jnp.dot(a, b, preferred_element_type=F32)


def dot_left(a, b):
    return lax.dot_general(a, b, (((0,), (0,)), ((), ())), preferred_element_type=F32)


def parts(value):
    first = value.astype(BF16).astype(F32)
    rest = value - first
    second = rest.astype(BF16).astype(F32)
    third = rest - second
    return first, second, third


def kernel(
    n_rep,
    n_slab,
    blocks,
    scales,
    listed,
    counts,
    partner,
    accept,
    positions,
    velocities,
    strength,
    inv_mass,
    solute,
    new_pos,
    new_vel,
    exponent,
    pick,
    pos8,
    vel8,
    feat8,
    own,
    far,
    flagged,
    acc,
    rows,
    stage,
    halo,
    state,
    swapped,
    energy,
    summary,
    halo_send,
    halo_recv,
    state_send,
    state_recv,
    energy_send,
    energy_recv,
    summary_send,
    summary_recv,
):
    rep = lax.axis_index("rep")
    here = lax.axis_index("slab")
    above = {"rep": lax.rem(rep + 1, n_rep)}
    below = {"rep": lax.rem(rep + n_rep - 1, n_rep)}
    after = {"slab": lax.rem(here + 1, n_slab)}
    before = {"slab": lax.rem(here + n_slab - 1, n_slab)}
    wide = blocks + 2 * RIM

    barrier = pltpu.get_barrier_semaphore()
    for other in range(1, n_slab):
        pl.semaphore_signal(
            barrier, 1, device_id={"slab": lax.rem(here + other, n_slab)}, device_id_type=MESH
        )
    for other in (below, above):
        pl.semaphore_signal(barrier, 1, device_id=other, device_id_type=MESH)

    row = lax.broadcasted_iota(jnp.int32, (8, 128), 0)
    long = (row == 0) | (row == 4)
    is3 = row == 3
    is7 = row == 7
    periods = (float(n_slab), BOX)
    inverse = jnp.where(long, F32(1.0 / periods[0]), F32(1.0 / periods[1]))
    phase = jnp.where(row >= 4, F32(0.25), F32(0.0))
    heights = [p * p / (2.0 * math.pi**2) / (2.0 * SIGMA**2) for p in periods]
    height = jnp.where(long, F32(heights[0]), F32(heights[1]))
    shift = heights[0] + 2.0 * heights[1]
    slope = jnp.where(
        long,
        F32(STEP * periods[0] / math.pi / (2.0 * SIGMA**2)),
        F32(STEP * periods[1] / math.pi / (2.0 * SIGMA**2)),
    )
    slope = jnp.where(is3 | is7, F32(0.0), jnp.where(row >= 4, -slope, slope))

    def features(x):
        turn = x * inverse - phase
        turn = turn - jnp.floor(turn + 0.5)
        w = 0.25 - jnp.abs(turn)
        z = w * w
        value = F32(SINE[-1])
        for c in SINE[-2::-1]:
            value = value * z + F32(c)
        return value * w

    def put_far(spot, value, log_weight):
        value = jnp.where(is3, F32(1.0), jnp.where(is7, log_weight, value))
        a, b, c = parts(value)
        far[spot] = jnp.concatenate([a, b, c, a, b, a], axis=0).astype(BF16)

    def put_own(b, value):
        value = jnp.where(is3, F32(-shift), jnp.where(is7, F32(1.0), value * height))
        x, y, z = parts(value)
        own[b] = jnp.concatenate([x, x, x, y, y, z], axis=0).astype(BF16)

    level = jnp.full((8, 128), scales[0], F32)
    root = jnp.sqrt(level)

    def atom_rows(t, carry):
        at = pl.ds(pl.multiple_of(t * 8, 8), 8)
        plain = strength[at, :]
        chosen = solute[at, :] == 1
        scaled = plain * jnp.where(chosen, root, F32(1.0))
        rows[0, at, :] = jnp.log(scaled)
        rows[1, at, :] = jnp.log(plain)
        rows[2, at, :] = jnp.where(chosen, F32(1.0), F32(0.0))
        rows[3, at, :] = scaled * inv_mass[at, :]
        return carry

    lax.fori_loop(0, blocks // 8, atom_rows, 0)

    def one_row(which, b):
        return rows[which, pl.ds(b, 1), :]

    def put_stage(turn, side, i, x, extra):
        stage[turn, side, i] = jnp.where(is3, extra, x)[:4]

    def load(b):
        blank = jnp.zeros((1, 128), F32)
        x = positions[pl.ds(b, 3, stride=blocks), :]
        v = velocities[pl.ds(b, 3, stride=blocks), :]
        pos8[b] = jnp.concatenate([x, blank, x, blank], axis=0)
        vel8[b] = jnp.concatenate([v, blank, v, blank], axis=0)

    def load_some(t, carry):
        for u in range(4):
            load(t * 4 + u)
        return carry

    lax.fori_loop(0, blocks // 4, load_some, 0)

    def stage_first(i, carry):
        low = i
        high = blocks - RIM + i
        put_stage(0, 0, i, pos8[low], one_row(0, low))
        put_stage(0, 1, i, pos8[high], one_row(0, high))
        return carry

    lax.fori_loop(0, RIM, stage_first, 0)
    pl.semaphore_wait(barrier, n_slab - 1 + 2)

    def halo_copy(turn, side):
        return pltpu.make_async_remote_copy(
            src_ref=stage.at[turn, side],
            dst_ref=halo.at[turn, side],
            send_sem=halo_send.at[turn, side],
            recv_sem=halo_recv.at[turn, side],
            device_id=before if side == 0 else after,
            device_id_type=MESH,
        )

    def send_halo(turn):
        for side in range(2):
            halo_copy(turn, side).start()

    send_halo(0)

    first = here * blocks
    total = n_slab * blocks

    def find(b, carry):
        count = counts[b]
        for k in range(1, NB):
            near = listed[k, b] - first
            near = jnp.where(near < 0, near + total, near)
            near = jnp.where(near < blocks + RIM, near, near - (total - blocks - 2 * RIM))
            pick[b * NB + k] = jnp.where(k < count, near, wide)
        return carry

    lax.fori_loop(0, blocks, find, 0)

    far[wide] = jnp.concatenate(
        [jnp.where(is7, F32(NONE), F32(0.0)), jnp.zeros((40, 128), F32)], axis=0
    ).astype(BF16)

    def own_features(which):
        def some(t, carry):
            for u in range(4):
                b = t * 4 + u
                value = features(pos8[b])
                feat8[b] = value
                put_own(b, value)
                put_far(b, value, one_row(which, b))
            return carry

        lax.fori_loop(0, blocks // 4, some, 0)

    def halo_features(turn):
        log_turn = 1 if turn == 2 else 0

        def some(t, carry):
            for side in range(2):
                for u in range(2):
                    i = t * 2 + u
                    got = halo[turn, side, i]
                    value = features(jnp.concatenate([got, got], axis=0))
                    put_far(blocks + side * RIM + i, value, halo[log_turn, side, i][3:4])
                    if turn == 2:
                        put_flags(blocks + side * RIM + i, got[3:4])
            return carry

        lax.fori_loop(0, RIM // 2, some, 0)

    def put_flags(spot, flags):
        flagged[spot] = jnp.where(
            lax.broadcasted_iota(jnp.int32, (16, 128), 0) == 0, flags, F32(1.0)
        ).astype(BF16)

    def sums(columns, picks, b):
        ahead = jnp.concatenate([far[n] for n in picks], axis=1)
        values = jnp.exp(dot_left(ahead, own[b]))
        weights = jnp.concatenate([columns(n) for n in picks], axis=1)
        high = values.astype(BF16)
        low = (values - high.astype(F32)).astype(BF16)
        return dot(weights, high) + dot(weights, low)

    def force_columns(n):
        return far[n, :32, :]

    def force_sums(picks, b):
        found = sums(force_columns, picks, b)
        return found[0:8] + found[8:16] + found[16:24]

    def self_pass(amount, one):
        def some(t, carry):
            found = [one([t * amount + u], t * amount + u) for u in range(amount)]
            for u in range(amount):
                acc[t * amount + u] = found[u]
            return carry

        lax.fori_loop(0, blocks // amount, some, 0)

    def move(b, found):
        value = feat8[b]
        found = found * pltpu.roll(value, 4, 0)
        found = found - pltpu.roll(found, 4, 0)
        vel = vel8[b] + slope * one_row(3, b) * found
        pos = pos8[b] + F32(STEP) * vel
        return pos, vel

    def picks_of(b):
        return [pick[b * NB + k] for k in range(1, NB)]

    def force_pass(turn):
        def rim(t, carry):
            spots = [t * 4 + u for u in range(4)] + [blocks - RIM + t * 4 + u for u in range(4)]
            found = [force_sums(picks_of(b), b) for b in spots]
            for u, b in enumerate(spots):
                pos, vel = move(b, found[u] + acc[b])
                keep(turn, b, pos, vel)
                put_stage(turn + 1, u // 4, t * 4 + u % 4, pos, one_row(1 + turn, b))
            return carry

        lax.fori_loop(0, RIM // 4, rim, 0)
        send_halo(turn + 1)

        def inner(t, carry):
            spots = [RIM + t * 8 + u for u in range(8)]
            found = [force_sums(picks_of(b), b) for b in spots]
            for u, b in enumerate(spots):
                pos, vel = move(b, found[u] + acc[b])
                keep(turn, b, pos, vel)
            return carry

        lax.fori_loop(0, (blocks - 2 * RIM) // 8, inner, 0)

    def keep(turn, b, pos, vel):
        pos8[b] = pos
        if turn == 0:
            vel8[b] = vel
        else:
            state[pl.ds(b, 3, stride=blocks), :] = pos[:3]
            state[pl.ds(3 * blocks + b, 3, stride=blocks), :] = vel[:3]

    def state_copy(side):
        return pltpu.make_async_remote_copy(
            src_ref=state,
            dst_ref=swapped.at[side],
            send_sem=state_send.at[side],
            recv_sem=state_recv.at[side],
            device_id=above if side == 0 else below,
            device_id_type=MESH,
        )

    def finish_halo(turn):
        for side in range(2):
            halo_copy(turn, side).wait()

    for turn in range(2):
        own_features(0)
        self_pass(8, force_sums)
        finish_halo(turn)
        halo_features(turn)
        force_pass(turn)

    state_copy(0).start()
    state_copy(1).start()

    own_features(1)

    def own_flags(b, carry):
        put_flags(b, one_row(2, b))
        return carry

    lax.fori_loop(0, blocks, own_flags, 0)
    flagged[wide] = jnp.zeros((16, 128), BF16)

    def energy_columns(n):
        return flagged[n]

    def energy_sums(picks, b):
        return sums(energy_columns, picks, b)[:8]

    self_pass(8, energy_sums)
    finish_halo(2)
    halo_features(2)

    def energies(t, carry):
        spots = [t * 8 + u for u in range(8)]
        found = [energy_sums(picks_of(b), b) for b in spots]
        inside_sum, mixed_sum = carry
        for u, b in enumerate(spots):
            both = found[u] + acc[b]
            inside = both[0:1]
            every = both[1:2]
            flags = one_row(2, b)
            plain = strength[pl.ds(b, 1), :]
            inside_sum = inside_sum + plain * flags * inside
            mixed_sum = mixed_sum + plain * (
                flags * (every - inside) + (F32(1.0) - flags) * inside
            )
        return inside_sum, mixed_sum

    blank = jnp.zeros((1, 128), F32)
    inside_sum, mixed_sum = lax.fori_loop(0, blocks // 8, energies, (blank, blank))
    mine = jnp.where(row == 0, inside_sum, jnp.where(row == 1, mixed_sum, F32(0.0)))
    energy[here] = mine

    def energy_copy(other, slot):
        return pltpu.make_async_remote_copy(
            src_ref=energy.at[here],
            dst_ref=energy.at[slot],
            send_sem=energy_send.at[other],
            recv_sem=energy_recv.at[slot],
            device_id={"slab": lax.rem(here + other, n_slab)},
            device_id_type=MESH,
        )

    for other in range(1, n_slab):
        energy_copy(other, here).start()

    mate = partner[0]
    taken = accept[0] == 1
    from_below = jnp.full((8, 128), jnp.where(taken & (mate == rep - 1), 1, 0)) == 1
    from_above = jnp.full((8, 128), jnp.where(taken & (mate == rep + 1), 1, 0)) == 1
    for side in range(2):
        state_copy(side).wait()
    for kind, result in ((0, new_pos), (1, new_vel)):

        def choose(t, carry):
            at = pl.ds(pl.multiple_of(t * 8, 8), 8)
            held = pl.ds(pl.multiple_of(3 * kind * blocks + t * 8, 8), 8)
            value = jnp.where(from_below, swapped[0, held, :], state[held, :])
            result[at, :] = jnp.where(from_above, swapped[1, held, :], value)
            return carry

        lax.fori_loop(0, 3 * blocks // 8, choose, 0)

    for other in range(1, n_slab):
        energy_copy(other, lax.rem(here + other, n_slab)).wait_recv()
    every = energy[0]
    for slot in range(1, n_slab):
        every = every + energy[slot]
    every = 0.5 * jnp.sum(every, axis=1, keepdims=True)
    every = jnp.where(row == 2, level, jnp.broadcast_to(every, (8, 128)))
    summary[2] = every

    def summary_copy(side):
        return pltpu.make_async_remote_copy(
            src_ref=summary.at[2],
            dst_ref=summary.at[side],
            send_sem=summary_send.at[side],
            recv_sem=summary_recv.at[side],
            device_id=above if side == 0 else below,
            device_id_type=MESH,
        )

    summary_copy(0).start()
    summary_copy(1).start()
    for other in range(1, n_slab):
        energy_copy(other, here).wait_send()
    summary_copy(0).wait()
    summary_copy(1).wait()
    is_below = jnp.full((8, 128), jnp.where(mate == rep - 1, 1, 0)) == 1
    is_above = jnp.full((8, 128), jnp.where(mate == rep + 1, 1, 0)) == 1
    theirs = jnp.where(is_below, summary[0], jnp.where(is_above, summary[1], every))
    gap = every - theirs
    far_level = theirs[2:3]
    near_level = every[2:3]
    answer = (far_level - near_level) * gap[0:1] + (
        jnp.sqrt(far_level) - jnp.sqrt(near_level)
    ) * gap[1:2]
    answer = answer / F32(total * 128)
    exponent[0] = answer[0, 0]


def shards(
    positions, velocities, strength, inv_mass, solute, scales, neighbours, counts, partner, accept
):
    n_rep = lax.axis_size("rep")
    n_slab = lax.axis_size("slab")
    atoms = positions.shape[2]
    blocks = atoms // 128
    wide = blocks + 2 * RIM
    pairs = 3 * blocks * NB * 128 * 128
    smem = pl.BlockSpec(memory_space=pltpu.SMEM)
    vmem = pl.BlockSpec(memory_space=pltpu.VMEM)
    rowed = (blocks, 128)
    new_pos, new_vel, exponent = pl.pallas_call(
        functools.partial(kernel, n_rep, n_slab, blocks),
        out_shape=(
            jax.ShapeDtypeStruct((3 * blocks, 128), F32),
            jax.ShapeDtypeStruct((3 * blocks, 128), F32),
            jax.ShapeDtypeStruct((1,), F32),
        ),
        in_specs=[smem] * 5 + [vmem] * 5,
        out_specs=(vmem, vmem, smem),
        scratch_shapes=[
            pltpu.SMEM((blocks * NB,), jnp.int32),
            pltpu.VMEM((blocks, 8, 128), F32),
            pltpu.VMEM((blocks, 8, 128), F32),
            pltpu.VMEM((blocks, 8, 128), F32),
            pltpu.VMEM((blocks, 48, 128), BF16),
            pltpu.VMEM((wide + 1, 48, 128), BF16),
            pltpu.VMEM((wide + 1, 16, 128), BF16),
            pltpu.VMEM((blocks, 8, 128), F32),
            pltpu.VMEM((4, blocks, 128), F32),
            pltpu.VMEM((3, 2, RIM, 4, 128), F32),
            pltpu.VMEM((3, 2, RIM, 4, 128), F32),
            pltpu.VMEM((6 * blocks, 128), F32),
            pltpu.VMEM((2, 6 * blocks, 128), F32),
            pltpu.VMEM((n_slab, 8, 128), F32),
            pltpu.VMEM((3, 8, 128), F32),
            pltpu.SemaphoreType.DMA((3, 2)),
            pltpu.SemaphoreType.DMA((3, 2)),
            pltpu.SemaphoreType.DMA((2,)),
            pltpu.SemaphoreType.DMA((2,)),
            pltpu.SemaphoreType.DMA((n_slab,)),
            pltpu.SemaphoreType.DMA((n_slab,)),
            pltpu.SemaphoreType.DMA((2,)),
            pltpu.SemaphoreType.DMA((2,)),
        ],
        compiler_params=pltpu.CompilerParams(
            collective_id=0, has_side_effects=True, vmem_limit_bytes=32 << 20
        ),
        cost_estimate=pl.CostEstimate(
            flops=pairs * 100, bytes_accessed=1 << 20, transcendentals=pairs
        ),
    )(
        scales,
        neighbours.T,
        counts,
        partner,
        accept,
        positions.reshape(3 * blocks, 128),
        velocities.reshape(3 * blocks, 128),
        strength.reshape(rowed),
        inv_mass.reshape(rowed),
        solute.reshape(rowed),
    )
    shape = positions.shape
    return (new_pos.reshape(shape), new_vel.reshape(shape), exponent)


def solution(mesh):
    placed = (
        P("rep", None, "slab"),
        P("rep", None, "slab"),
        P("slab"),
        P("slab"),
        P("slab"),
        P("rep"),
        P("slab", None),
        P("slab"),
        P("rep"),
        P("rep"),
    )
    return jax.shard_map(
        shards,
        mesh=mesh,
        in_specs=placed,
        out_specs=(P("rep", None, "slab"), P("rep", None, "slab"), P("rep")),
        check_vma=False,
    )
```

```python
import functools
import math

import jax
import jax.numpy as jnp
from jax import lax
from jax.experimental import pallas as pl
from jax.experimental.pallas import tpu as pltpu
from jax.sharding import PartitionSpec as P

NB = 4
RIM = 16
SIGMA = 0.35
BOX = 2.0
STEP = 0.02
NONE = -1000.0
MESH = pl.DeviceIdType.MESH
F32 = jnp.float32
BF16 = jnp.bfloat16
SINE = (
    6.28318530717,
    -41.34170211,
    81.60522621,
    -76.70428132,
    42.00980576,
    -14.39413556,
)


def dot(a, b):
    return jnp.dot(a, b, preferred_element_type=F32)


def dot_left(a, b):
    return lax.dot_general(a, b, (((0,), (0,)), ((), ())), preferred_element_type=F32)


def parts(value):
    first = value.astype(BF16).astype(F32)
    rest = value - first
    second = rest.astype(BF16).astype(F32)
    third = rest - second
    return first, second, third


def kernel(
    n_rep,
    n_slab,
    blocks,
    scales_far,
    listed_far,
    counts_far,
    partner_far,
    accept_far,
    positions_far,
    velocities_far,
    strength_far,
    inv_mass_far,
    solute_far,
    new_pos,
    new_vel,
    exponent,
    scales,
    listed,
    counts,
    partner,
    accept,
    positions,
    velocities,
    strength,
    inv_mass,
    solute,
    fetch,
    pick,
    pos8,
    vel8,
    feat8,
    own,
    far,
    flagged,
    acc,
    rows,
    stage,
    halo,
    state,
    swapped,
    energy,
    summary,
    halo_send,
    halo_recv,
    state_send,
    state_recv,
    energy_send,
    energy_recv,
    summary_send,
    summary_recv,
):
    rep = lax.axis_index("rep")
    here = lax.axis_index("slab")
    above = {"rep": lax.rem(rep + 1, n_rep)}
    below = {"rep": lax.rem(rep + n_rep - 1, n_rep)}
    after = {"slab": lax.rem(here + 1, n_slab)}
    before = {"slab": lax.rem(here + n_slab - 1, n_slab)}
    wide = blocks + 2 * RIM

    fetches = [
        pltpu.make_async_copy(source, target, fetch.at[i])
        for i, (source, target) in enumerate(
            (
                (strength_far, strength),
                (solute_far, solute),
                (inv_mass_far, inv_mass),
                (scales_far, scales),
                (positions_far, positions),
                (velocities_far, velocities),
                (listed_far, listed),
                (counts_far, counts),
                (partner_far, partner),
                (accept_far, accept),
            )
        )
    ]
    for copy in fetches:
        copy.start()
    barrier = pltpu.get_barrier_semaphore()
    for other in range(1, n_slab):
        pl.semaphore_signal(
            barrier, 1, device_id={"slab": lax.rem(here + other, n_slab)}, device_id_type=MESH
        )
    for other in (below, above):
        pl.semaphore_signal(barrier, 1, device_id=other, device_id_type=MESH)

    row = lax.broadcasted_iota(jnp.int32, (8, 128), 0)
    long = (row == 0) | (row == 4)
    is3 = row == 3
    is7 = row == 7
    periods = (float(n_slab), BOX)
    inverse = jnp.where(long, F32(1.0 / periods[0]), F32(1.0 / periods[1]))
    phase = jnp.where(row >= 4, F32(0.25), F32(0.0))
    heights = [p * p / (2.0 * math.pi**2) / (2.0 * SIGMA**2) for p in periods]
    height = jnp.where(long, F32(math.sqrt(heights[0])), F32(math.sqrt(heights[1])))
    shift = heights[0] + 2.0 * heights[1]
    slope = [STEP * p / math.pi / (2.0 * SIGMA**2) / h for p, h in zip(periods, heights)]
    slope = jnp.where(long, F32(slope[0]), F32(slope[1]))
    slope = jnp.where(is3 | is7, F32(0.0), jnp.where(row >= 4, -slope, slope))

    def features(x):
        turn = x * inverse - phase
        turn = turn - jnp.floor(turn + 0.5)
        w = 0.25 - jnp.abs(turn)
        z = w * w
        value = F32(SINE[-1])
        for c in SINE[-2::-1]:
            value = value * z + F32(c)
        return value * (w * height)

    fixed = parts(jnp.where(is3, F32(-shift), F32(1.0)))

    def put(spot, value, log_weight, owned):
        value = jnp.where(is3, F32(1.0), jnp.where(is7, log_weight, value))
        a, b, c = parts(value)
        far[spot] = jnp.concatenate([a, b, c, a, b, a], axis=0).astype(BF16)
        if owned:
            x, y, z = [jnp.where(is3 | is7, k, v) for k, v in zip(fixed, (a, b, c))]
            own[spot] = jnp.concatenate([x, x, x, y, y, z], axis=0).astype(BF16)

    for copy in fetches:
        copy.wait()

    level = jnp.full((8, 128), scales[0], F32)
    root = jnp.sqrt(level)

    def atom_rows(t, carry):
        at = pl.ds(pl.multiple_of(t * 8, 8), 8)
        plain = strength[at, :]
        chosen = solute[at, :] == 1
        scaled = plain * jnp.where(chosen, root, F32(1.0))
        rows[0, at, :] = jnp.log(scaled)
        rows[1, at, :] = jnp.log(plain)
        rows[2, at, :] = jnp.where(chosen, F32(1.0), F32(0.0))
        rows[3, at, :] = scaled * inv_mass[at, :]
        return carry

    lax.fori_loop(0, blocks // 8, atom_rows, 0)

    def one_row(which, b):
        return rows[which, pl.ds(b, 1), :]

    def put_stage(turn, side, i, x, extra):
        stage[turn, side, i] = jnp.where(is3, extra, x)[:4]

    def load(b):
        blank = jnp.zeros((1, 128), F32)
        x = positions[pl.ds(b, 3, stride=blocks), :]
        v = velocities[pl.ds(b, 3, stride=blocks), :]
        pos8[b] = jnp.concatenate([x, blank, x, blank], axis=0)
        vel8[b] = jnp.concatenate([v, blank, v, blank], axis=0)

    def load_some(t, carry):
        for u in range(4):
            load(t * 4 + u)
        return carry

    lax.fori_loop(0, blocks // 4, load_some, 0)

    def stage_first(i, carry):
        low = i
        high = blocks - RIM + i
        put_stage(0, 0, i, pos8[low], one_row(0, low))
        put_stage(0, 1, i, pos8[high], one_row(0, high))
        return carry

    lax.fori_loop(0, RIM, stage_first, 0)
    pl.semaphore_wait(barrier, n_slab - 1 + 2)

    def halo_copy(turn, side):
        return pltpu.make_async_remote_copy(
            src_ref=stage.at[turn, side],
            dst_ref=halo.at[turn, side],
            send_sem=halo_send.at[turn, side],
            recv_sem=halo_recv.at[turn, side],
            device_id=before if side == 0 else after,
            device_id_type=MESH,
        )

    def send_halo(turn):
        for side in range(2):
            halo_copy(turn, side).start()

    send_halo(0)

    first = here * blocks
    total = n_slab * blocks

    def find(b, carry):
        count = counts[b]
        for k in range(1, NB):
            near = listed[k, b] - first
            near = jnp.where(near < 0, near + total, near)
            near = jnp.where(near < blocks + RIM, near, near - (total - blocks - 2 * RIM))
            pick[b * NB + k] = jnp.where(k < count, near, wide)
        return carry

    lax.fori_loop(0, blocks, find, 0)

    far[wide] = jnp.concatenate(
        [jnp.where(is7, F32(NONE), F32(0.0)), jnp.zeros((40, 128), F32)], axis=0
    ).astype(BF16)

    def own_features(which):
        def some(t, carry):
            for u in range(12):
                b = t * 12 + u
                value = features(pos8[b])
                feat8[b] = value
                put(b, value, one_row(which, b), True)
            return carry

        lax.fori_loop(0, blocks // 12, some, 0)

    def halo_features(turn):
        log_turn = 1 if turn == 2 else 0

        def some(t, carry):
            for side in range(2):
                for u in range(4):
                    i = t * 4 + u
                    got = halo[turn, side, i]
                    value = features(jnp.concatenate([got, got], axis=0))
                    put(blocks + side * RIM + i, value, halo[log_turn, side, i][3:4], False)
                    if turn == 2:
                        put_flags(blocks + side * RIM + i, got[3:4])
            return carry

        lax.fori_loop(0, RIM // 4, some, 0)

    def put_flags(spot, flags):
        flagged[spot] = jnp.where(
            lax.broadcasted_iota(jnp.int32, (16, 128), 0) == 0, flags, F32(1.0)
        ).astype(BF16)

    def exponents(picks, b):
        ahead = jnp.concatenate([far[n] for n in picks], axis=1)
        return dot_left(ahead, own[b])

    def sums(columns, picks, b, exps):
        values = jnp.exp(exps)
        weights = jnp.concatenate([columns(n) for n in picks], axis=1)
        high = values.astype(BF16)
        low = (values - high.astype(F32)).astype(BF16)
        return dot(weights, high) + dot(weights, low)

    def all_sums(one, picked):
        exps = [exponents(picks, b) for picks, b in picked]
        return [one(picks, b, y) for (picks, b), y in zip(picked, exps)]

    def force_columns(n):
        return far[n, :32, :]

    def force_sums(picks, b, exps):
        found = sums(force_columns, picks, b, exps)
        return found[0:8] + found[8:16] + found[16:24]

    def self_pass(amount, one):
        def some(t, carry):
            found = all_sums(one, [([t * amount + u], t * amount + u) for u in range(amount)])
            for u in range(amount):
                acc[t * amount + u] = found[u]
            return carry

        lax.fori_loop(0, blocks // amount, some, 0)

    def move(b, found):
        value = feat8[b]
        found = found * pltpu.roll(value, 4, 0)
        found = found - pltpu.roll(found, 4, 0)
        vel = vel8[b] + slope * one_row(3, b) * found
        pos = pos8[b] + F32(STEP) * vel
        return pos, vel

    def picks_of(b):
        return [pick[b * NB + k] for k in range(1, NB)]

    def force_pass(turn):
        def rim(t, carry):
            spots = [t * 8 + u for u in range(8)] + [blocks - RIM + t * 8 + u for u in range(8)]
            found = all_sums(force_sums, [(picks_of(b), b) for b in spots])
            for u, b in enumerate(spots):
                pos, vel = move(b, found[u] + acc[b])
                keep(turn, b, pos, vel)
                put_stage(turn + 1, u // 8, t * 8 + u % 8, pos, one_row(1 + turn, b))
            return carry

        lax.fori_loop(0, RIM // 8, rim, 0)
        send_halo(turn + 1)

        def inner(t, carry):
            spots = [RIM + t * 16 + u for u in range(16)]
            found = all_sums(force_sums, [(picks_of(b), b) for b in spots])
            for u, b in enumerate(spots):
                pos, vel = move(b, found[u] + acc[b])
                keep(turn, b, pos, vel)
            return carry

        lax.fori_loop(0, (blocks - 2 * RIM) // 16, inner, 0)

    def keep(turn, b, pos, vel):
        pos8[b] = pos
        if turn == 0:
            vel8[b] = vel
        else:
            state[pl.ds(b, 3, stride=blocks), :] = pos[:3]
            state[pl.ds(3 * blocks + b, 3, stride=blocks), :] = vel[:3]

    def state_copy(side):
        return pltpu.make_async_remote_copy(
            src_ref=state,
            dst_ref=swapped.at[side],
            send_sem=state_send.at[side],
            recv_sem=state_recv.at[side],
            device_id=above if side == 0 else below,
            device_id_type=MESH,
        )

    def finish_halo(turn):
        for side in range(2):
            halo_copy(turn, side).wait()

    for turn in range(2):
        own_features(0)
        self_pass(24, force_sums)
        finish_halo(turn)
        halo_features(turn)
        force_pass(turn)

    state_copy(0).start()
    state_copy(1).start()

    own_features(1)

    def own_flags(b, carry):
        put_flags(b, one_row(2, b))
        return carry

    lax.fori_loop(0, blocks, own_flags, 0)
    flagged[wide] = jnp.zeros((16, 128), BF16)

    def energy_columns(n):
        return flagged[n]

    def energy_sums(picks, b, exps):
        return sums(energy_columns, picks, b, exps)[:8]

    self_pass(24, energy_sums)
    finish_halo(2)
    halo_features(2)

    def energies(t, carry):
        spots = [t * 16 + u for u in range(16)]
        found = all_sums(energy_sums, [(picks_of(b), b) for b in spots])
        inside_sum, mixed_sum = carry
        for u, b in enumerate(spots):
            both = found[u] + acc[b]
            inside = both[0:1]
            every = both[1:2]
            flags = one_row(2, b)
            plain = strength[pl.ds(b, 1), :]
            inside_sum = inside_sum + plain * flags * inside
            mixed_sum = mixed_sum + plain * (
                flags * (every - inside) + (F32(1.0) - flags) * inside
            )
        return inside_sum, mixed_sum

    blank = jnp.zeros((1, 128), F32)
    inside_sum, mixed_sum = lax.fori_loop(0, blocks // 16, energies, (blank, blank))
    mine = jnp.where(row == 0, inside_sum, jnp.where(row == 1, mixed_sum, F32(0.0)))
    energy[here] = mine

    def energy_copy(other, slot):
        return pltpu.make_async_remote_copy(
            src_ref=energy.at[here],
            dst_ref=energy.at[slot],
            send_sem=energy_send.at[other],
            recv_sem=energy_recv.at[slot],
            device_id={"slab": lax.rem(here + other, n_slab)},
            device_id_type=MESH,
        )

    for other in range(1, n_slab):
        energy_copy(other, here).start()

    mate = partner[0]
    taken = accept[0] == 1
    from_below = jnp.full((8, 128), jnp.where(taken & (mate == rep - 1), 1, 0)) == 1
    from_above = jnp.full((8, 128), jnp.where(taken & (mate == rep + 1), 1, 0)) == 1
    for side in range(2):
        state_copy(side).wait()
    for kind, result in ((0, new_pos), (1, new_vel)):

        def choose(t, carry):
            at = pl.ds(pl.multiple_of(t * 8, 8), 8)
            held = pl.ds(pl.multiple_of(3 * kind * blocks + t * 8, 8), 8)
            value = jnp.where(from_below, swapped[0, held, :], state[held, :])
            result[at, :] = jnp.where(from_above, swapped[1, held, :], value)
            return carry

        lax.fori_loop(0, 3 * blocks // 8, choose, 0)

    for other in range(1, n_slab):
        energy_copy(other, lax.rem(here + other, n_slab)).wait_recv()
    every = energy[0]
    for slot in range(1, n_slab):
        every = every + energy[slot]
    every = 0.5 * jnp.sum(every, axis=1, keepdims=True)
    every = jnp.where(row == 2, level, jnp.broadcast_to(every, (8, 128)))
    summary[2] = every

    def summary_copy(side):
        return pltpu.make_async_remote_copy(
            src_ref=summary.at[2],
            dst_ref=summary.at[side],
            send_sem=summary_send.at[side],
            recv_sem=summary_recv.at[side],
            device_id=above if side == 0 else below,
            device_id_type=MESH,
        )

    summary_copy(0).start()
    summary_copy(1).start()
    for other in range(1, n_slab):
        energy_copy(other, here).wait_send()
    summary_copy(0).wait()
    summary_copy(1).wait()
    is_below = jnp.full((8, 128), jnp.where(mate == rep - 1, 1, 0)) == 1
    is_above = jnp.full((8, 128), jnp.where(mate == rep + 1, 1, 0)) == 1
    theirs = jnp.where(is_below, summary[0], jnp.where(is_above, summary[1], every))
    gap = every - theirs
    far_level = theirs[2:3]
    near_level = every[2:3]
    answer = (far_level - near_level) * gap[0:1] + (
        jnp.sqrt(far_level) - jnp.sqrt(near_level)
    ) * gap[1:2]
    answer = answer / F32(total * 128)
    exponent[0] = answer[0, 0]


def shards(
    positions, velocities, strength, inv_mass, solute, scales, neighbours, counts, partner, accept
):
    n_rep = lax.axis_size("rep")
    n_slab = lax.axis_size("slab")
    atoms = positions.shape[2]
    blocks = atoms // 128
    wide = blocks + 2 * RIM
    pairs = 3 * blocks * NB * 128 * 128
    smem = pl.BlockSpec(memory_space=pltpu.SMEM)
    vmem = pl.BlockSpec(memory_space=pltpu.VMEM)
    rowed = (blocks, 128)
    new_pos, new_vel, exponent = pl.pallas_call(
        functools.partial(kernel, n_rep, n_slab, blocks),
        out_shape=(
            jax.ShapeDtypeStruct((3 * blocks, 128), F32),
            jax.ShapeDtypeStruct((3 * blocks, 128), F32),
            jax.ShapeDtypeStruct((1,), F32),
        ),
        in_specs=[pl.BlockSpec(memory_space=pltpu.HBM)] * 10,
        out_specs=(vmem, vmem, smem),
        scratch_shapes=[
            pltpu.SMEM((1,), F32),
            pltpu.SMEM((NB, blocks), jnp.int32),
            pltpu.SMEM((blocks,), jnp.int32),
            pltpu.SMEM((1,), jnp.int32),
            pltpu.SMEM((1,), jnp.int32),
            pltpu.VMEM((3 * blocks, 128), F32),
            pltpu.VMEM((3 * blocks, 128), F32),
            pltpu.VMEM(rowed, F32),
            pltpu.VMEM(rowed, F32),
            pltpu.VMEM(rowed, jnp.int32),
            pltpu.SemaphoreType.DMA((10,)),
            pltpu.SMEM((blocks * NB,), jnp.int32),
            pltpu.VMEM((blocks, 8, 128), F32),
            pltpu.VMEM((blocks, 8, 128), F32),
            pltpu.VMEM((blocks, 8, 128), F32),
            pltpu.VMEM((blocks, 48, 128), BF16),
            pltpu.VMEM((wide + 1, 48, 128), BF16),
            pltpu.VMEM((wide + 1, 16, 128), BF16),
            pltpu.VMEM((blocks, 8, 128), F32),
            pltpu.VMEM((4, blocks, 128), F32),
            pltpu.VMEM((3, 2, RIM, 4, 128), F32),
            pltpu.VMEM((3, 2, RIM, 4, 128), F32),
            pltpu.VMEM((6 * blocks, 128), F32),
            pltpu.VMEM((2, 6 * blocks, 128), F32),
            pltpu.VMEM((n_slab, 8, 128), F32),
            pltpu.VMEM((3, 8, 128), F32),
            pltpu.SemaphoreType.DMA((3, 2)),
            pltpu.SemaphoreType.DMA((3, 2)),
            pltpu.SemaphoreType.DMA((2,)),
            pltpu.SemaphoreType.DMA((2,)),
            pltpu.SemaphoreType.DMA((n_slab,)),
            pltpu.SemaphoreType.DMA((n_slab,)),
            pltpu.SemaphoreType.DMA((2,)),
            pltpu.SemaphoreType.DMA((2,)),
        ],
        compiler_params=pltpu.CompilerParams(
            collective_id=0, has_side_effects=True, vmem_limit_bytes=56 << 20
        ),
        cost_estimate=pl.CostEstimate(
            flops=pairs * 100, bytes_accessed=1 << 20, transcendentals=pairs
        ),
    )(
        scales,
        neighbours.T,
        counts,
        partner,
        accept,
        positions.reshape(3 * blocks, 128),
        velocities.reshape(3 * blocks, 128),
        strength.reshape(rowed),
        inv_mass.reshape(rowed),
        solute.reshape(rowed),
    )
    shape = positions.shape
    return (new_pos.reshape(shape), new_vel.reshape(shape), exponent)


def solution(mesh):
    placed = (
        P("rep", None, "slab"),
        P("rep", None, "slab"),
        P("slab"),
        P("slab"),
        P("slab"),
        P("rep"),
        P("slab", None),
        P("slab"),
        P("rep"),
        P("rep"),
    )
    return jax.shard_map(
        shards,
        mesh=mesh,
        in_specs=placed,
        out_specs=(P("rep", None, "slab"), P("rep", None, "slab"), P("rep")),
        check_vma=False,
    )
```

```python
import functools
import math

import jax
import jax.numpy as jnp
from jax import lax
from jax.experimental import pallas as pl
from jax.experimental.pallas import tpu as pltpu
from jax.sharding import PartitionSpec as P

NB = 4
RIM = 16
SIGMA = 0.35
BOX = 2.0
STEP = 0.02
NONE = -1000.0
MESH = pl.DeviceIdType.MESH
F32 = jnp.float32
BF16 = jnp.bfloat16
SINE = (
    6.28318530717,
    -41.34170211,
    81.60522621,
    -76.70428132,
    42.00980576,
    -14.39413556,
)


def dot(a, b):
    return jnp.dot(a, b, preferred_element_type=F32)


def dot_left(a, b):
    return lax.dot_general(a, b, (((0,), (0,)), ((), ())), preferred_element_type=F32)


def parts(value):
    first = value.astype(BF16).astype(F32)
    rest = value - first
    second = rest.astype(BF16).astype(F32)
    third = rest - second
    return first, second, third


def kernel(
    n_rep,
    n_slab,
    blocks,
    scales_far,
    listed_far,
    counts_far,
    partner_far,
    accept_far,
    positions_far,
    velocities_far,
    strength_far,
    inv_mass_far,
    solute_far,
    new_pos,
    new_vel,
    exponent,
    scales,
    listed,
    counts,
    partner,
    accept,
    positions,
    velocities,
    strength,
    inv_mass,
    solute,
    fetch,
    pick,
    pos8,
    vel8,
    feat8,
    own,
    far,
    flagged,
    acc,
    rows,
    stage,
    halo,
    state,
    swapped,
    energy,
    summary,
    halo_send,
    halo_recv,
    state_send,
    state_recv,
    energy_send,
    energy_recv,
    summary_send,
    summary_recv,
):
    rep = lax.axis_index("rep")
    here = lax.axis_index("slab")
    above = {"rep": jnp.minimum(rep + 1, n_rep - 1)}
    below = {"rep": jnp.maximum(rep - 1, 0)}
    after = {"slab": lax.rem(here + 1, n_slab)}
    before = {"slab": lax.rem(here + n_slab - 1, n_slab)}
    wide = blocks + 2 * RIM

    fetches = [
        pltpu.make_async_copy(source, target, fetch.at[i])
        for i, (source, target) in enumerate(
            (
                (strength_far, strength),
                (solute_far, solute),
                (inv_mass_far, inv_mass),
                (scales_far, scales),
                (positions_far, positions),
                (velocities_far, velocities),
                (listed_far, listed),
                (counts_far, counts),
                (partner_far, partner),
                (accept_far, accept),
            )
        )
    ]
    for copy in fetches:
        copy.start()
    barrier = pltpu.get_barrier_semaphore()
    for other in range(1, n_slab):
        pl.semaphore_signal(
            barrier, 1, device_id={"slab": lax.rem(here + other, n_slab)}, device_id_type=MESH
        )
    has_below = rep > 0
    has_above = rep < n_rep - 1

    @pl.when(has_below)
    def _():
        pl.semaphore_signal(barrier, 1, device_id=below, device_id_type=MESH)

    @pl.when(has_above)
    def _():
        pl.semaphore_signal(barrier, 1, device_id=above, device_id_type=MESH)


    row = lax.broadcasted_iota(jnp.int32, (8, 128), 0)
    long = (row == 0) | (row == 4)
    is3 = row == 3
    is7 = row == 7
    periods = (float(n_slab), BOX)
    inverse = jnp.where(long, F32(1.0 / periods[0]), F32(1.0 / periods[1]))
    phase = jnp.where(row >= 4, F32(0.25), F32(0.0))
    heights = [p * p / (2.0 * math.pi**2) / (2.0 * SIGMA**2) for p in periods]
    height = jnp.where(long, F32(math.sqrt(heights[0])), F32(math.sqrt(heights[1])))
    shift = heights[0] + 2.0 * heights[1]
    slope = [STEP * p / math.pi / (2.0 * SIGMA**2) / h for p, h in zip(periods, heights)]
    slope = jnp.where(long, F32(slope[0]), F32(slope[1]))
    slope = jnp.where(is3 | is7, F32(0.0), jnp.where(row >= 4, -slope, slope))

    def features(x):
        turn = x * inverse - phase
        turn = turn - jnp.floor(turn + 0.5)
        w = 0.25 - jnp.abs(turn)
        z = w * w
        value = F32(SINE[-1])
        for c in SINE[-2::-1]:
            value = value * z + F32(c)
        return value * (w * height)

    fixed = parts(jnp.where(is3, F32(-shift), F32(1.0)))

    def put(spot, value, log_weight, owned):
        value = jnp.where(is3, F32(1.0), jnp.where(is7, log_weight, value))
        a, b, c = parts(value)
        far[spot] = jnp.concatenate([a, b, c, a, b, a], axis=0).astype(BF16)
        if owned:
            x, y, z = [jnp.where(is3 | is7, k, v) for k, v in zip(fixed, (a, b, c))]
            own[spot] = jnp.concatenate([x, x, x, y, y, z], axis=0).astype(BF16)

    for copy in fetches:
        copy.wait()

    level = jnp.full((8, 128), scales[0], F32)
    root = jnp.sqrt(level)

    def atom_rows(t, carry):
        at = pl.ds(pl.multiple_of(t * 8, 8), 8)
        plain = strength[at, :]
        chosen = solute[at, :] == 1
        scaled = plain * jnp.where(chosen, root, F32(1.0))
        rows[0, at, :] = jnp.log(scaled)
        rows[1, at, :] = jnp.log(plain)
        rows[2, at, :] = jnp.where(chosen, F32(1.0), F32(0.0))
        rows[3, at, :] = scaled * inv_mass[at, :]
        return carry

    lax.fori_loop(0, blocks // 8, atom_rows, 0)

    def one_row(which, b):
        return rows[which, pl.ds(b, 1), :]

    def put_stage(turn, side, i, x, extra):
        stage[turn, side, i] = jnp.where(is3, extra, x)[:4]

    def load(b):
        blank = jnp.zeros((1, 128), F32)
        x = positions[pl.ds(b, 3, stride=blocks), :]
        v = velocities[pl.ds(b, 3, stride=blocks), :]
        pos8[b] = jnp.concatenate([x, blank, x, blank], axis=0)
        vel8[b] = jnp.concatenate([v, blank, v, blank], axis=0)

    def load_some(t, carry):
        for u in range(4):
            load(t * 4 + u)
        return carry

    lax.fori_loop(0, blocks // 4, load_some, 0)

    def stage_first(i, carry):
        low = i
        high = blocks - RIM + i
        put_stage(0, 0, i, pos8[low], one_row(0, low))
        put_stage(0, 1, i, pos8[high], one_row(0, high))
        return carry

    lax.fori_loop(0, RIM, stage_first, 0)
    pl.semaphore_wait(barrier, n_slab - 1 + has_below.astype(jnp.int32) + has_above.astype(jnp.int32))

    def halo_copy(turn, side):
        return pltpu.make_async_remote_copy(
            src_ref=stage.at[turn, side],
            dst_ref=halo.at[turn, side],
            send_sem=halo_send.at[turn, side],
            recv_sem=halo_recv.at[turn, side],
            device_id=before if side == 0 else after,
            device_id_type=MESH,
        )

    def send_halo(turn):
        for side in range(2):
            halo_copy(turn, side).start()

    send_halo(0)

    first = here * blocks
    total = n_slab * blocks

    def find(b, carry):
        count = counts[b]
        for k in range(1, NB):
            near = listed[k, b] - first
            near = jnp.where(near < 0, near + total, near)
            near = jnp.where(near < blocks + RIM, near, near - (total - blocks - 2 * RIM))
            pick[b * NB + k] = jnp.where(k < count, near, wide)
        return carry

    lax.fori_loop(0, blocks, find, 0)

    far[wide] = jnp.concatenate(
        [jnp.where(is7, F32(NONE), F32(0.0)), jnp.zeros((40, 128), F32)], axis=0
    ).astype(BF16)

    def own_features(which):
        def some(t, carry):
            for u in range(12):
                b = t * 12 + u
                value = features(pos8[b])
                feat8[b] = value
                put(b, value, one_row(which, b), True)
            return carry

        lax.fori_loop(0, blocks // 12, some, 0)

    def halo_features(turn):
        log_turn = 1 if turn == 2 else 0

        def some(t, carry):
            for side in range(2):
                for u in range(4):
                    i = t * 4 + u
                    got = halo[turn, side, i]
                    value = features(jnp.concatenate([got, got], axis=0))
                    put(blocks + side * RIM + i, value, halo[log_turn, side, i][3:4], False)
                    if turn == 2:
                        put_flags(blocks + side * RIM + i, got[3:4])
            return carry

        lax.fori_loop(0, RIM // 4, some, 0)

    def put_flags(spot, flags):
        flagged[spot] = jnp.where(
            lax.broadcasted_iota(jnp.int32, (16, 128), 0) == 0, flags, F32(1.0)
        ).astype(BF16)

    def exponents(picks, b):
        ahead = jnp.concatenate([far[n] for n in picks], axis=1)
        return dot_left(ahead, own[b])

    def sums(columns, picks, b, exps):
        values = jnp.exp(exps)
        weights = jnp.concatenate([columns(n) for n in picks], axis=1)
        high = values.astype(BF16)
        low = (values - high.astype(F32)).astype(BF16)
        return dot(weights, high) + dot(weights, low)

    def all_sums(one, picked):
        exps = [exponents(picks, b) for picks, b in picked]
        return [one(picks, b, y) for (picks, b), y in zip(picked, exps)]

    def force_columns(n):
        return far[n, :32, :]

    def force_sums(picks, b, exps):
        found = sums(force_columns, picks, b, exps)
        return found[0:8] + found[8:16] + found[16:24]

    def self_pass(amount, one):
        def some(t, carry):
            found = all_sums(one, [([t * amount + u], t * amount + u) for u in range(amount)])
            for u in range(amount):
                acc[t * amount + u] = found[u]
            return carry

        lax.fori_loop(0, blocks // amount, some, 0)

    def move(b, found):
        value = feat8[b]
        found = found * pltpu.roll(value, 4, 0)
        found = found - pltpu.roll(found, 4, 0)
        vel = vel8[b] + slope * one_row(3, b) * found
        pos = pos8[b] + F32(STEP) * vel
        return pos, vel

    def picks_of(b):
        return [pick[b * NB + k] for k in range(1, NB)]

    def force_pass(turn):
        def rim(t, carry):
            spots = [t * 8 + u for u in range(8)] + [blocks - RIM + t * 8 + u for u in range(8)]
            found = all_sums(force_sums, [(picks_of(b), b) for b in spots])
            for u, b in enumerate(spots):
                pos, vel = move(b, found[u] + acc[b])
                keep(turn, b, pos, vel)
                put_stage(turn + 1, u // 8, t * 8 + u % 8, pos, one_row(1 + turn, b))
            return carry

        lax.fori_loop(0, RIM // 8, rim, 0)
        send_halo(turn + 1)

        def inner(t, carry):
            spots = [RIM + t * 16 + u for u in range(16)]
            found = all_sums(force_sums, [(picks_of(b), b) for b in spots])
            for u, b in enumerate(spots):
                pos, vel = move(b, found[u] + acc[b])
                keep(turn, b, pos, vel)
            return carry

        lax.fori_loop(0, (blocks - 2 * RIM) // 16, inner, 0)

    def keep(turn, b, pos, vel):
        pos8[b] = pos
        if turn == 0:
            vel8[b] = vel
        else:
            state[pl.ds(b, 3, stride=blocks), :] = pos[:3]
            state[pl.ds(3 * blocks + b, 3, stride=blocks), :] = vel[:3]

    def state_copy(side):
        return pltpu.make_async_remote_copy(
            src_ref=state,
            dst_ref=swapped.at[side],
            send_sem=state_send.at[side],
            recv_sem=state_recv.at[side],
            device_id=above if side == 0 else below,
            device_id_type=MESH,
        )

    def finish_halo(turn):
        for side in range(2):
            halo_copy(turn, side).wait()

    for turn in range(2):
        own_features(0)
        self_pass(24, force_sums)
        finish_halo(turn)
        halo_features(turn)
        force_pass(turn)

    def start_pair(copy):
        pl.when(has_above)(lambda: copy(0).start())
        pl.when(has_below)(lambda: copy(1).start())

    def wait_pair(copy):
        @pl.when(has_above)
        def _():
            copy(0).wait_send()
            copy(1).wait_recv()

        @pl.when(has_below)
        def _():
            copy(1).wait_send()
            copy(0).wait_recv()

    start_pair(state_copy)

    own_features(1)

    def own_flags(b, carry):
        put_flags(b, one_row(2, b))
        return carry

    lax.fori_loop(0, blocks, own_flags, 0)
    flagged[wide] = jnp.zeros((16, 128), BF16)

    def energy_columns(n):
        return flagged[n]

    def energy_sums(picks, b, exps):
        return sums(energy_columns, picks, b, exps)[:8]

    self_pass(24, energy_sums)
    finish_halo(2)
    halo_features(2)

    def energies(t, carry):
        spots = [t * 16 + u for u in range(16)]
        found = all_sums(energy_sums, [(picks_of(b), b) for b in spots])
        inside_sum, mixed_sum = carry
        for u, b in enumerate(spots):
            both = found[u] + acc[b]
            inside = both[0:1]
            every = both[1:2]
            flags = one_row(2, b)
            plain = strength[pl.ds(b, 1), :]
            inside_sum = inside_sum + plain * flags * inside
            mixed_sum = mixed_sum + plain * (
                flags * (every - inside) + (F32(1.0) - flags) * inside
            )
        return inside_sum, mixed_sum

    blank = jnp.zeros((1, 128), F32)
    inside_sum, mixed_sum = lax.fori_loop(0, blocks // 16, energies, (blank, blank))
    mine = jnp.where(row == 0, inside_sum, jnp.where(row == 1, mixed_sum, F32(0.0)))
    energy[here] = mine

    def energy_copy(other, slot):
        return pltpu.make_async_remote_copy(
            src_ref=energy.at[here],
            dst_ref=energy.at[slot],
            send_sem=energy_send.at[other],
            recv_sem=energy_recv.at[slot],
            device_id={"slab": lax.rem(here + other, n_slab)},
            device_id_type=MESH,
        )

    for other in range(1, n_slab):
        energy_copy(other, here).start()

    mate = partner[0]
    taken = accept[0] == 1
    from_below = jnp.full((8, 128), jnp.where(taken & (mate == rep - 1), 1, 0)) == 1
    from_above = jnp.full((8, 128), jnp.where(taken & (mate == rep + 1), 1, 0)) == 1
    wait_pair(state_copy)
    for kind, result in ((0, new_pos), (1, new_vel)):

        def choose(t, carry):
            at = pl.ds(pl.multiple_of(t * 8, 8), 8)
            held = pl.ds(pl.multiple_of(3 * kind * blocks + t * 8, 8), 8)
            value = jnp.where(from_below, swapped[0, held, :], state[held, :])
            result[at, :] = jnp.where(from_above, swapped[1, held, :], value)
            return carry

        lax.fori_loop(0, 3 * blocks // 8, choose, 0)

    for other in range(1, n_slab):
        energy_copy(other, lax.rem(here + other, n_slab)).wait_recv()
    every = energy[0]
    for slot in range(1, n_slab):
        every = every + energy[slot]
    every = 0.5 * jnp.sum(every, axis=1, keepdims=True)
    every = jnp.where(row == 2, level, jnp.broadcast_to(every, (8, 128)))
    summary[2] = every

    def summary_copy(side):
        return pltpu.make_async_remote_copy(
            src_ref=summary.at[2],
            dst_ref=summary.at[side],
            send_sem=summary_send.at[side],
            recv_sem=summary_recv.at[side],
            device_id=above if side == 0 else below,
            device_id_type=MESH,
        )

    start_pair(summary_copy)
    for other in range(1, n_slab):
        energy_copy(other, here).wait_send()
    wait_pair(summary_copy)
    is_below = jnp.full((8, 128), jnp.where(mate == rep - 1, 1, 0)) == 1
    is_above = jnp.full((8, 128), jnp.where(mate == rep + 1, 1, 0)) == 1
    theirs = jnp.where(is_below, summary[0], jnp.where(is_above, summary[1], every))
    gap = every - theirs
    far_level = theirs[2:3]
    near_level = every[2:3]
    answer = (far_level - near_level) * gap[0:1] + (
        jnp.sqrt(far_level) - jnp.sqrt(near_level)
    ) * gap[1:2]
    answer = answer / F32(total * 128)
    exponent[0] = answer[0, 0]


def shards(
    positions, velocities, strength, inv_mass, solute, scales, neighbours, counts, partner, accept
):
    n_rep = lax.axis_size("rep")
    n_slab = lax.axis_size("slab")
    atoms = positions.shape[2]
    blocks = atoms // 128
    wide = blocks + 2 * RIM
    pairs = 3 * blocks * NB * 128 * 128
    smem = pl.BlockSpec(memory_space=pltpu.SMEM)
    vmem = pl.BlockSpec(memory_space=pltpu.VMEM)
    rowed = (blocks, 128)
    new_pos, new_vel, exponent = pl.pallas_call(
        functools.partial(kernel, n_rep, n_slab, blocks),
        out_shape=(
            jax.ShapeDtypeStruct((3 * blocks, 128), F32),
            jax.ShapeDtypeStruct((3 * blocks, 128), F32),
            jax.ShapeDtypeStruct((1,), F32),
        ),
        in_specs=[pl.BlockSpec(memory_space=pltpu.HBM)] * 10,
        out_specs=(vmem, vmem, smem),
        scratch_shapes=[
            pltpu.SMEM((1,), F32),
            pltpu.SMEM((NB, blocks), jnp.int32),
            pltpu.SMEM((blocks,), jnp.int32),
            pltpu.SMEM((1,), jnp.int32),
            pltpu.SMEM((1,), jnp.int32),
            pltpu.VMEM((3 * blocks, 128), F32),
            pltpu.VMEM((3 * blocks, 128), F32),
            pltpu.VMEM(rowed, F32),
            pltpu.VMEM(rowed, F32),
            pltpu.VMEM(rowed, jnp.int32),
            pltpu.SemaphoreType.DMA((10,)),
            pltpu.SMEM((blocks * NB,), jnp.int32),
            pltpu.VMEM((blocks, 8, 128), F32),
            pltpu.VMEM((blocks, 8, 128), F32),
            pltpu.VMEM((blocks, 8, 128), F32),
            pltpu.VMEM((blocks, 48, 128), BF16),
            pltpu.VMEM((wide + 1, 48, 128), BF16),
            pltpu.VMEM((wide + 1, 16, 128), BF16),
            pltpu.VMEM((blocks, 8, 128), F32),
            pltpu.VMEM((4, blocks, 128), F32),
            pltpu.VMEM((3, 2, RIM, 4, 128), F32),
            pltpu.VMEM((3, 2, RIM, 4, 128), F32),
            pltpu.VMEM((6 * blocks, 128), F32),
            pltpu.VMEM((2, 6 * blocks, 128), F32),
            pltpu.VMEM((n_slab, 8, 128), F32),
            pltpu.VMEM((3, 8, 128), F32),
            pltpu.SemaphoreType.DMA((3, 2)),
            pltpu.SemaphoreType.DMA((3, 2)),
            pltpu.SemaphoreType.DMA((2,)),
            pltpu.SemaphoreType.DMA((2,)),
            pltpu.SemaphoreType.DMA((n_slab,)),
            pltpu.SemaphoreType.DMA((n_slab,)),
            pltpu.SemaphoreType.DMA((2,)),
            pltpu.SemaphoreType.DMA((2,)),
        ],
        compiler_params=pltpu.CompilerParams(
            collective_id=0, has_side_effects=True, vmem_limit_bytes=56 << 20
        ),
        cost_estimate=pl.CostEstimate(
            flops=pairs * 100, bytes_accessed=1 << 20, transcendentals=pairs
        ),
    )(
        scales,
        neighbours.T,
        counts,
        partner,
        accept,
        positions.reshape(3 * blocks, 128),
        velocities.reshape(3 * blocks, 128),
        strength.reshape(rowed),
        inv_mass.reshape(rowed),
        solute.reshape(rowed),
    )
    shape = positions.shape
    return (new_pos.reshape(shape), new_vel.reshape(shape), exponent)


def solution(mesh):
    placed = (
        P("rep", None, "slab"),
        P("rep", None, "slab"),
        P("slab"),
        P("slab"),
        P("slab"),
        P("rep"),
        P("slab", None),
        P("slab"),
        P("rep"),
        P("rep"),
    )
    return jax.shard_map(
        shards,
        mesh=mesh,
        in_specs=placed,
        out_specs=(P("rep", None, "slab"), P("rep", None, "slab"), P("rep")),
        check_vma=False,
    )
```

```python
import functools
import math

import jax
import jax.numpy as jnp
from jax import lax
from jax.experimental import pallas as pl
from jax.experimental.pallas import tpu as pltpu
from jax.sharding import PartitionSpec as P

NB = 4
RIM = 16
SIGMA = 0.35
BOX = 2.0
STEP = 0.02
NONE = -1000.0
MESH = pl.DeviceIdType.MESH
F32 = jnp.float32
BF16 = jnp.bfloat16
SINE = (
    6.28318530717,
    -41.34170211,
    81.60522621,
    -76.70428132,
    42.00980576,
    -14.39413556,
)


def dot(a, b):
    return jnp.dot(a, b, preferred_element_type=F32)


def dot_left(a, b):
    return lax.dot_general(a, b, (((0,), (0,)), ((), ())), preferred_element_type=F32)


def parts(value):
    first = value.astype(BF16).astype(F32)
    rest = value - first
    second = rest.astype(BF16).astype(F32)
    third = rest - second
    return first, second, third


def kernel(
    n_rep,
    n_slab,
    blocks,
    scales_far,
    listed_far,
    counts_far,
    partner_far,
    accept_far,
    positions_far,
    velocities_far,
    strength_far,
    inv_mass_far,
    solute_far,
    new_pos,
    new_vel,
    exponent,
    scales,
    listed,
    counts,
    partner,
    accept,
    positions,
    velocities,
    strength,
    inv_mass,
    solute,
    fetch,
    pick,
    pos8,
    vel8,
    feat8,
    own,
    far,
    flagged,
    acc,
    rows,
    stage,
    halo,
    state,
    swapped,
    energy,
    halo_send,
    halo_recv,
    state_send,
    state_recv,
    energy_send,
    energy_recv,
):
    rep = lax.axis_index("rep")
    here = lax.axis_index("slab")
    above = {"rep": jnp.minimum(rep + 1, n_rep - 1)}
    below = {"rep": jnp.maximum(rep - 1, 0)}
    after = {"slab": lax.rem(here + 1, n_slab)}
    before = {"slab": lax.rem(here + n_slab - 1, n_slab)}
    wide = blocks + 2 * RIM

    fetches = [
        pltpu.make_async_copy(source, target, fetch.at[i])
        for i, (source, target) in enumerate(
            (
                (strength_far, strength),
                (solute_far, solute),
                (inv_mass_far, inv_mass),
                (scales_far, scales),
                (positions_far, positions),
                (velocities_far, velocities),
                (listed_far, listed),
                (counts_far, counts),
                (partner_far, partner),
                (accept_far, accept),
            )
        )
    ]
    for copy in fetches:
        copy.start()
    barrier = pltpu.get_barrier_semaphore()
    has_below = rep > 0
    has_above = rep < n_rep - 1

    def mate_slab(line, other):
        return {**line, "slab": lax.rem(here + other, n_slab)}

    def greet(line, start):
        for other in range(start, n_slab):
            pl.semaphore_signal(
                barrier, 1, device_id=mate_slab(line, other), device_id_type=MESH
            )

    greet({}, 1)
    pl.when(has_below)(lambda: greet(below, 0))
    pl.when(has_above)(lambda: greet(above, 0))

    row = lax.broadcasted_iota(jnp.int32, (8, 128), 0)
    long = (row == 0) | (row == 4)
    is3 = row == 3
    is7 = row == 7
    periods = (float(n_slab), BOX)
    inverse = jnp.where(long, F32(1.0 / periods[0]), F32(1.0 / periods[1]))
    phase = jnp.where(row >= 4, F32(0.25), F32(0.0))
    heights = [p * p / (2.0 * math.pi**2) / (2.0 * SIGMA**2) for p in periods]
    height = jnp.where(long, F32(math.sqrt(heights[0])), F32(math.sqrt(heights[1])))
    shift = heights[0] + 2.0 * heights[1]
    slope = [STEP * p / math.pi / (2.0 * SIGMA**2) / h for p, h in zip(periods, heights)]
    slope = jnp.where(long, F32(slope[0]), F32(slope[1]))
    slope = jnp.where(is3 | is7, F32(0.0), jnp.where(row >= 4, -slope, slope))

    def features(x):
        turn = x * inverse - phase
        turn = turn - jnp.floor(turn + 0.5)
        w = 0.25 - jnp.abs(turn)
        z = w * w
        value = F32(SINE[-1])
        for c in SINE[-2::-1]:
            value = value * z + F32(c)
        return value * (w * height)

    fixed = parts(jnp.where(is3, F32(-shift), F32(1.0)))

    def put(spot, value, log_weight, owned):
        value = jnp.where(is3, F32(1.0), jnp.where(is7, log_weight, value))
        a, b, c = parts(value)
        far[spot] = jnp.concatenate([a, b, c, a, b, a], axis=0).astype(BF16)
        if owned:
            x, y, z = [jnp.where(is3 | is7, k, v) for k, v in zip(fixed, (a, b, c))]
            own[spot] = jnp.concatenate([x, x, x, y, y, z], axis=0).astype(BF16)

    for copy in fetches:
        copy.wait()

    level = jnp.full((8, 128), scales[0], F32)
    root = jnp.sqrt(level)

    def atom_rows(t, carry):
        at = pl.ds(pl.multiple_of(t * 8, 8), 8)
        plain = strength[at, :]
        chosen = solute[at, :] == 1
        scaled = plain * jnp.where(chosen, root, F32(1.0))
        rows[0, at, :] = jnp.log(scaled)
        rows[1, at, :] = jnp.log(plain)
        rows[2, at, :] = jnp.where(chosen, F32(1.0), F32(0.0))
        rows[3, at, :] = scaled * inv_mass[at, :]
        return carry

    lax.fori_loop(0, blocks // 8, atom_rows, 0)

    def one_row(which, b):
        return rows[which, pl.ds(b, 1), :]

    def put_stage(turn, side, i, x, extra):
        stage[turn, side, i] = jnp.where(is3, extra, x)[:4]

    def load(b):
        blank = jnp.zeros((1, 128), F32)
        x = positions[pl.ds(b, 3, stride=blocks), :]
        v = velocities[pl.ds(b, 3, stride=blocks), :]
        pos8[b] = jnp.concatenate([x, blank, x, blank], axis=0)
        vel8[b] = jnp.concatenate([v, blank, v, blank], axis=0)

    def load_some(t, carry):
        for u in range(4):
            load(t * 4 + u)
        return carry

    lax.fori_loop(0, blocks // 4, load_some, 0)

    def stage_first(i, carry):
        low = i
        high = blocks - RIM + i
        put_stage(0, 0, i, pos8[low], one_row(0, low))
        put_stage(0, 1, i, pos8[high], one_row(0, high))
        return carry

    lax.fori_loop(0, RIM, stage_first, 0)
    lines = has_below.astype(jnp.int32) + has_above.astype(jnp.int32)
    pl.semaphore_wait(barrier, n_slab - 1 + n_slab * lines)

    def halo_copy(turn, side):
        return pltpu.make_async_remote_copy(
            src_ref=stage.at[turn, side],
            dst_ref=halo.at[turn, side],
            send_sem=halo_send.at[turn, side],
            recv_sem=halo_recv.at[turn, side],
            device_id=before if side == 0 else after,
            device_id_type=MESH,
        )

    def send_halo(turn):
        for side in range(2):
            halo_copy(turn, side).start()

    send_halo(0)

    first = here * blocks
    total = n_slab * blocks

    def find(b, carry):
        count = counts[b]
        for k in range(1, NB):
            near = listed[k, b] - first
            near = jnp.where(near < 0, near + total, near)
            near = jnp.where(near < blocks + RIM, near, near - (total - blocks - 2 * RIM))
            pick[b * NB + k] = jnp.where(k < count, near, wide)
        return carry

    lax.fori_loop(0, blocks, find, 0)

    far[wide] = jnp.concatenate(
        [jnp.where(is7, F32(NONE), F32(0.0)), jnp.zeros((40, 128), F32)], axis=0
    ).astype(BF16)

    def own_features(which):
        def some(t, carry):
            for u in range(12):
                b = t * 12 + u
                value = features(pos8[b])
                feat8[b] = value
                put(b, value, one_row(which, b), True)
            return carry

        lax.fori_loop(0, blocks // 12, some, 0)

    def halo_features(turn):
        log_turn = 1 if turn == 2 else 0

        def some(t, carry):
            for side in range(2):
                for u in range(4):
                    i = t * 4 + u
                    got = halo[turn, side, i]
                    value = features(jnp.concatenate([got, got], axis=0))
                    put(blocks + side * RIM + i, value, halo[log_turn, side, i][3:4], False)
                    if turn == 2:
                        put_flags(blocks + side * RIM + i, got[3:4])
            return carry

        lax.fori_loop(0, RIM // 4, some, 0)

    def put_flags(spot, flags):
        flagged[spot] = jnp.where(
            lax.broadcasted_iota(jnp.int32, (16, 128), 0) == 0, flags, F32(1.0)
        ).astype(BF16)

    def exponents(picks, b):
        ahead = jnp.concatenate([far[n] for n in picks], axis=1)
        return dot_left(ahead, own[b])

    def sums(columns, picks, b, exps):
        values = jnp.exp(exps)
        weights = jnp.concatenate([columns(n) for n in picks], axis=1)
        high = values.astype(BF16)
        low = (values - high.astype(F32)).astype(BF16)
        return dot(weights, high) + dot(weights, low)

    def all_sums(one, picked):
        exps = [exponents(picks, b) for picks, b in picked]
        return [one(picks, b, y) for (picks, b), y in zip(picked, exps)]

    def force_columns(n):
        return far[n, :32, :]

    def force_sums(picks, b, exps):
        found = sums(force_columns, picks, b, exps)
        return found[0:8] + found[8:16] + found[16:24]

    def self_pass(amount, one):
        def some(t, carry):
            found = all_sums(one, [([t * amount + u], t * amount + u) for u in range(amount)])
            for u in range(amount):
                acc[t * amount + u] = found[u]
            return carry

        lax.fori_loop(0, blocks // amount, some, 0)

    def move(b, found):
        value = feat8[b]
        found = found * pltpu.roll(value, 4, 0)
        found = found - pltpu.roll(found, 4, 0)
        vel = vel8[b] + slope * one_row(3, b) * found
        pos = pos8[b] + F32(STEP) * vel
        return pos, vel

    def picks_of(b):
        return [pick[b * NB + k] for k in range(1, NB)]

    def force_pass(turn):
        def rim(t, carry):
            spots = [t * 8 + u for u in range(8)] + [blocks - RIM + t * 8 + u for u in range(8)]
            found = all_sums(force_sums, [(picks_of(b), b) for b in spots])
            for u, b in enumerate(spots):
                pos, vel = move(b, found[u] + acc[b])
                keep(turn, b, pos, vel)
                put_stage(turn + 1, u // 8, t * 8 + u % 8, pos, one_row(1 + turn, b))
            return carry

        lax.fori_loop(0, RIM // 8, rim, 0)
        send_halo(turn + 1)

        def inner(t, carry):
            spots = [RIM + t * 16 + u for u in range(16)]
            found = all_sums(force_sums, [(picks_of(b), b) for b in spots])
            for u, b in enumerate(spots):
                pos, vel = move(b, found[u] + acc[b])
                keep(turn, b, pos, vel)
            return carry

        lax.fori_loop(0, (blocks - 2 * RIM) // 16, inner, 0)

    def keep(turn, b, pos, vel):
        pos8[b] = pos
        if turn == 0:
            vel8[b] = vel
        else:
            state[pl.ds(b, 3, stride=blocks), :] = pos[:3]
            state[pl.ds(3 * blocks + b, 3, stride=blocks), :] = vel[:3]

    def state_copy(side):
        return pltpu.make_async_remote_copy(
            src_ref=state,
            dst_ref=swapped.at[side],
            send_sem=state_send.at[side],
            recv_sem=state_recv.at[side],
            device_id=above if side == 0 else below,
            device_id_type=MESH,
        )

    def finish_halo(turn):
        for side in range(2):
            halo_copy(turn, side).wait()

    for turn in range(2):
        own_features(0)
        self_pass(24, force_sums)
        finish_halo(turn)
        halo_features(turn)
        force_pass(turn)

    def start_pair(copy):
        pl.when(has_above)(lambda: copy(0).start())
        pl.when(has_below)(lambda: copy(1).start())

    def wait_pair(copy):
        @pl.when(has_above)
        def _():
            copy(0).wait_send()
            copy(1).wait_recv()

        @pl.when(has_below)
        def _():
            copy(1).wait_send()
            copy(0).wait_recv()

    start_pair(state_copy)

    own_features(1)

    def own_flags(b, carry):
        put_flags(b, one_row(2, b))
        return carry

    lax.fori_loop(0, blocks, own_flags, 0)
    flagged[wide] = jnp.zeros((16, 128), BF16)

    def energy_columns(n):
        return flagged[n]

    def energy_sums(picks, b, exps):
        return sums(energy_columns, picks, b, exps)[:8]

    self_pass(24, energy_sums)
    finish_halo(2)
    halo_features(2)

    def energies(t, carry):
        spots = [t * 16 + u for u in range(16)]
        found = all_sums(energy_sums, [(picks_of(b), b) for b in spots])
        inside_sum, mixed_sum = carry
        for u, b in enumerate(spots):
            both = found[u] + acc[b]
            inside = both[0:1]
            every = both[1:2]
            flags = one_row(2, b)
            plain = strength[pl.ds(b, 1), :]
            inside_sum = inside_sum + plain * flags * inside
            mixed_sum = mixed_sum + plain * (
                flags * (every - inside) + (F32(1.0) - flags) * inside
            )
        return inside_sum, mixed_sum

    blank = jnp.zeros((1, 128), F32)
    inside_sum, mixed_sum = lax.fori_loop(0, blocks // 16, energies, (blank, blank))
    mine = jnp.where(row == 0, inside_sum, jnp.where(row == 1, mixed_sum, level))
    energy[2, here] = mine

    def energy_copy(kind, other, slot):
        line = above if kind == 0 else below if kind == 1 else {}
        return pltpu.make_async_remote_copy(
            src_ref=energy.at[2, here],
            dst_ref=energy.at[kind, slot],
            send_sem=energy_send.at[kind, other],
            recv_sem=energy_recv.at[kind, slot],
            device_id=mate_slab(line, other),
            device_id_type=MESH,
        )

    def send_energy(kind, start):
        for other in range(start, n_slab):
            energy_copy(kind, other, here).start()

    def receive_energy(kind, start):
        for other in range(start, n_slab):
            energy_copy(kind, other, lax.rem(here + other, n_slab)).wait_recv()

    def sent_energy(kind, start):
        for other in range(start, n_slab):
            energy_copy(kind, other, here).wait_send()

    pl.when(has_above)(lambda: send_energy(0, 0))
    pl.when(has_below)(lambda: send_energy(1, 0))
    send_energy(2, 1)

    mate = partner[0]
    taken = accept[0] == 1
    from_below = jnp.full((8, 128), jnp.where(taken & (mate == rep - 1), 1, 0)) == 1
    from_above = jnp.full((8, 128), jnp.where(taken & (mate == rep + 1), 1, 0)) == 1
    wait_pair(state_copy)
    for kind, result in ((0, new_pos), (1, new_vel)):

        def choose(t, carry):
            at = pl.ds(pl.multiple_of(t * 8, 8), 8)
            held = pl.ds(pl.multiple_of(3 * kind * blocks + t * 8, 8), 8)
            value = jnp.where(from_below, swapped[0, held, :], state[held, :])
            result[at, :] = jnp.where(from_above, swapped[1, held, :], value)
            return carry

        lax.fori_loop(0, 3 * blocks // 8, choose, 0)

    pl.when(has_above)(lambda: sent_energy(0, 0))
    pl.when(has_below)(lambda: sent_energy(1, 0))
    sent_energy(2, 1)
    receive_energy(2, 1)
    pl.when(has_below)(lambda: receive_energy(0, 0))
    pl.when(has_above)(lambda: receive_energy(1, 0))

    def whole(kind):
        every = energy[kind, 0]
        for slot in range(1, n_slab):
            every = every + energy[kind, slot]
        every = 0.5 * jnp.sum(every, axis=1, keepdims=True)
        return jnp.where(row == 2, energy[kind, 0], jnp.broadcast_to(every, (8, 128)))

    every = whole(2)
    is_below = jnp.full((8, 128), jnp.where(mate == rep - 1, 1, 0)) == 1
    is_above = jnp.full((8, 128), jnp.where(mate == rep + 1, 1, 0)) == 1
    theirs = jnp.where(is_below, whole(0), jnp.where(is_above, whole(1), every))
    gap = every - theirs
    far_level = theirs[2:3]
    near_level = every[2:3]
    answer = (far_level - near_level) * gap[0:1] + (
        jnp.sqrt(far_level) - jnp.sqrt(near_level)
    ) * gap[1:2]
    answer = answer / F32(total * 128)
    exponent[...] = jnp.broadcast_to(answer, (8, 128))


def shards(
    positions, velocities, strength, inv_mass, solute, scales, neighbours, counts, partner, accept
):
    n_rep = lax.axis_size("rep")
    n_slab = lax.axis_size("slab")
    atoms = positions.shape[2]
    blocks = atoms // 128
    wide = blocks + 2 * RIM
    pairs = 3 * blocks * NB * 128 * 128
    smem = pl.BlockSpec(memory_space=pltpu.SMEM)
    vmem = pl.BlockSpec(memory_space=pltpu.VMEM)
    rowed = (blocks, 128)
    new_pos, new_vel, exponent = pl.pallas_call(
        functools.partial(kernel, n_rep, n_slab, blocks),
        out_shape=(
            jax.ShapeDtypeStruct((3 * blocks, 128), F32),
            jax.ShapeDtypeStruct((3 * blocks, 128), F32),
            jax.ShapeDtypeStruct((8, 128), F32),
        ),
        in_specs=[pl.BlockSpec(memory_space=pltpu.HBM)] * 10,
        out_specs=(vmem, vmem, vmem),
        scratch_shapes=[
            pltpu.SMEM((1,), F32),
            pltpu.SMEM((NB, blocks), jnp.int32),
            pltpu.SMEM((blocks,), jnp.int32),
            pltpu.SMEM((1,), jnp.int32),
            pltpu.SMEM((1,), jnp.int32),
            pltpu.VMEM((3 * blocks, 128), F32),
            pltpu.VMEM((3 * blocks, 128), F32),
            pltpu.VMEM(rowed, F32),
            pltpu.VMEM(rowed, F32),
            pltpu.VMEM(rowed, jnp.int32),
            pltpu.SemaphoreType.DMA((10,)),
            pltpu.SMEM((blocks * NB,), jnp.int32),
            pltpu.VMEM((blocks, 8, 128), F32),
            pltpu.VMEM((blocks, 8, 128), F32),
            pltpu.VMEM((blocks, 8, 128), F32),
            pltpu.VMEM((blocks, 48, 128), BF16),
            pltpu.VMEM((wide + 1, 48, 128), BF16),
            pltpu.VMEM((wide + 1, 16, 128), BF16),
            pltpu.VMEM((blocks, 8, 128), F32),
            pltpu.VMEM((4, blocks, 128), F32),
            pltpu.VMEM((3, 2, RIM, 4, 128), F32),
            pltpu.VMEM((3, 2, RIM, 4, 128), F32),
            pltpu.VMEM((6 * blocks, 128), F32),
            pltpu.VMEM((2, 6 * blocks, 128), F32),
            pltpu.VMEM((3, n_slab, 8, 128), F32),
            pltpu.SemaphoreType.DMA((3, 2)),
            pltpu.SemaphoreType.DMA((3, 2)),
            pltpu.SemaphoreType.DMA((2,)),
            pltpu.SemaphoreType.DMA((2,)),
            pltpu.SemaphoreType.DMA((3, n_slab)),
            pltpu.SemaphoreType.DMA((3, n_slab)),
        ],
        compiler_params=pltpu.CompilerParams(
            collective_id=0, has_side_effects=True, vmem_limit_bytes=56 << 20
        ),
        cost_estimate=pl.CostEstimate(
            flops=pairs * 100, bytes_accessed=1 << 20, transcendentals=pairs
        ),
    )(
        scales,
        neighbours.T,
        counts,
        partner,
        accept,
        positions.reshape(3 * blocks, 128),
        velocities.reshape(3 * blocks, 128),
        strength.reshape(rowed),
        inv_mass.reshape(rowed),
        solute.reshape(rowed),
    )
    shape = positions.shape
    return (new_pos.reshape(shape), new_vel.reshape(shape), exponent[0, :1])


def solution(mesh):
    placed = (
        P("rep", None, "slab"),
        P("rep", None, "slab"),
        P("slab"),
        P("slab"),
        P("slab"),
        P("rep"),
        P("slab", None),
        P("slab"),
        P("rep"),
        P("rep"),
    )
    return jax.shard_map(
        shards,
        mesh=mesh,
        in_specs=placed,
        out_specs=(P("rep", None, "slab"), P("rep", None, "slab"), P("rep")),
        check_vma=False,
    )
```

```python
import functools
import math

import jax
import jax.numpy as jnp
from jax import lax
from jax.experimental import pallas as pl
from jax.experimental.pallas import tpu as pltpu
from jax.sharding import PartitionSpec as P

NB = 4
RIM = 16
SIGMA = 0.35
BOX = 2.0
STEP = 0.02
NONE = -1000.0
MESH = pl.DeviceIdType.MESH
F32 = jnp.float32
BF16 = jnp.bfloat16
SINE = (
    6.28318530717,
    -41.34170211,
    81.60522621,
    -76.70428132,
    42.00980576,
    -14.39413556,
)


def dot(a, b):
    return jnp.dot(a, b, preferred_element_type=F32)


def dot_left(a, b):
    return lax.dot_general(a, b, (((0,), (0,)), ((), ())), preferred_element_type=F32)


def parts(value):
    first = value.astype(BF16).astype(F32)
    rest = value - first
    second = rest.astype(BF16).astype(F32)
    third = rest - second
    return first, second, third


def kernel(
    n_rep,
    n_slab,
    blocks,
    scales_far,
    listed_far,
    counts_far,
    partner_far,
    accept_far,
    positions_far,
    velocities_far,
    strength_far,
    inv_mass_far,
    solute_far,
    new_pos,
    new_vel,
    exponent,
    scales,
    listed,
    counts,
    partner,
    accept,
    positions,
    velocities,
    strength,
    inv_mass,
    solute,
    fetch,
    pick,
    pos8,
    vel8,
    feat8,
    own,
    far,
    flagged,
    acc,
    rows,
    stage,
    halo,
    state,
    swapped,
    energy,
    halo_send,
    halo_recv,
    state_send,
    state_recv,
    energy_send,
    energy_recv,
):
    rep = lax.axis_index("rep")
    here = lax.axis_index("slab")
    above = {"rep": jnp.minimum(rep + 1, n_rep - 1)}
    below = {"rep": jnp.maximum(rep - 1, 0)}
    after = {"slab": lax.rem(here + 1, n_slab)}
    before = {"slab": lax.rem(here + n_slab - 1, n_slab)}
    wide = blocks + 2 * RIM

    fetches = [
        pltpu.make_async_copy(source, target, fetch.at[i])
        for i, (source, target) in enumerate(
            (
                (strength_far, strength),
                (solute_far, solute),
                (inv_mass_far, inv_mass),
                (scales_far, scales),
                (positions_far, positions),
                (velocities_far, velocities),
                (listed_far, listed),
                (counts_far, counts),
                (partner_far, partner),
                (accept_far, accept),
            )
        )
    ]
    for copy in fetches:
        copy.start()
    barrier = pltpu.get_barrier_semaphore()
    has_below = rep > 0
    has_above = rep < n_rep - 1

    def mate_slab(line, other):
        return {**line, "slab": lax.rem(here + other, n_slab)}

    def greet(line, start):
        for other in range(start, n_slab):
            pl.semaphore_signal(
                barrier, 1, device_id=mate_slab(line, other), device_id_type=MESH
            )

    greet({}, 1)
    pl.when(has_below)(lambda: greet(below, 0))
    pl.when(has_above)(lambda: greet(above, 0))

    row = lax.broadcasted_iota(jnp.int32, (8, 128), 0)
    long = (row == 0) | (row == 4)
    is3 = row == 3
    is7 = row == 7
    periods = (float(n_slab), BOX)
    inverse = jnp.where(long, F32(1.0 / periods[0]), F32(1.0 / periods[1]))
    phase = jnp.where(row >= 4, F32(0.25), F32(0.0))
    heights = [p * p / (2.0 * math.pi**2) / (2.0 * SIGMA**2) for p in periods]
    height = jnp.where(long, F32(math.sqrt(heights[0])), F32(math.sqrt(heights[1])))
    shift = heights[0] + 2.0 * heights[1]
    slope = [STEP * p / math.pi / (2.0 * SIGMA**2) / h for p, h in zip(periods, heights)]
    slope = jnp.where(long, F32(slope[0]), F32(slope[1]))
    slope = jnp.where(is3 | is7, F32(0.0), jnp.where(row >= 4, -slope, slope))

    def features(x):
        turn = x * inverse - phase
        turn = turn - jnp.floor(turn + 0.5)
        w = 0.25 - jnp.abs(turn)
        z = w * w
        value = F32(SINE[-1])
        for c in SINE[-2::-1]:
            value = value * z + F32(c)
        return value * (w * height)

    fixed = parts(jnp.where(is3, F32(-shift), F32(1.0)))

    def put(spot, value, log_weight, owned):
        value = jnp.where(is3, F32(1.0), jnp.where(is7, log_weight, value))
        a, b, c = parts(value)
        far[spot] = jnp.concatenate([a, b, c, a, b, a], axis=0).astype(BF16)
        if owned:
            x, y, z = [jnp.where(is3 | is7, k, v) for k, v in zip(fixed, (a, b, c))]
            own[spot] = jnp.concatenate([x, x, x, y, y, z], axis=0).astype(BF16)

    for copy in fetches:
        copy.wait()

    level = jnp.full((8, 128), scales[0], F32)
    root = jnp.sqrt(level)

    def atom_rows(t, carry):
        at = pl.ds(pl.multiple_of(t * 8, 8), 8)
        plain = strength[at, :]
        chosen = solute[at, :] == 1
        scaled = plain * jnp.where(chosen, root, F32(1.0))
        rows[0, at, :] = jnp.log(scaled)
        rows[1, at, :] = jnp.log(plain)
        rows[2, at, :] = jnp.where(chosen, F32(1.0), F32(0.0))
        rows[3, at, :] = scaled * inv_mass[at, :]
        return carry

    lax.fori_loop(0, blocks // 8, atom_rows, 0)

    def one_row(which, b):
        return rows[which, pl.ds(b, 1), :]

    def put_stage(turn, side, i, x, extra):
        stage[turn, side, i] = jnp.where(is3, extra, x)[:4]

    def load(b):
        blank = jnp.zeros((1, 128), F32)
        x = positions[pl.ds(b, 3, stride=blocks), :]
        v = velocities[pl.ds(b, 3, stride=blocks), :]
        pos8[b] = jnp.concatenate([x, blank, x, blank], axis=0)
        vel8[b] = jnp.concatenate([v, blank, v, blank], axis=0)

    def load_some(t, carry):
        for u in range(4):
            load(t * 4 + u)
        return carry

    lax.fori_loop(0, blocks // 4, load_some, 0)

    def stage_first(i, carry):
        low = i
        high = blocks - RIM + i
        put_stage(0, 0, i, pos8[low], one_row(0, low))
        put_stage(0, 1, i, pos8[high], one_row(0, high))
        return carry

    lax.fori_loop(0, RIM, stage_first, 0)
    lines = has_below.astype(jnp.int32) + has_above.astype(jnp.int32)
    pl.semaphore_wait(barrier, n_slab - 1 + n_slab * lines)

    def halo_copy(turn, side):
        return pltpu.make_async_remote_copy(
            src_ref=stage.at[turn, side],
            dst_ref=halo.at[turn, side],
            send_sem=halo_send.at[turn, side],
            recv_sem=halo_recv.at[turn, side],
            device_id=before if side == 0 else after,
            device_id_type=MESH,
        )

    def send_halo(turn):
        for side in range(2):
            halo_copy(turn, side).start()

    send_halo(0)

    first = here * blocks
    total = n_slab * blocks

    def find(b, carry):
        count = counts[b]
        for k in range(1, NB):
            near = listed[k, b] - first
            near = jnp.where(near < 0, near + total, near)
            near = jnp.where(near < blocks + RIM, near, near - (total - blocks - 2 * RIM))
            pick[b * NB + k] = jnp.where(k < count, near, wide)
        return carry

    lax.fori_loop(0, blocks, find, 0)

    far[wide] = jnp.concatenate(
        [jnp.where(is7, F32(NONE), F32(0.0)), jnp.zeros((40, 128), F32)], axis=0
    ).astype(BF16)

    def own_features(which):
        def some(t, carry):
            for u in range(12):
                b = t * 12 + u
                value = features(pos8[b])
                feat8[b] = value
                put(b, value, one_row(which, b), True)
            return carry

        lax.fori_loop(0, blocks // 12, some, 0)

    def halo_features(turn):
        log_turn = 1 if turn == 2 else 0

        def some(t, carry):
            for side in range(2):
                for u in range(4):
                    i = t * 4 + u
                    got = halo[turn, side, i]
                    value = features(jnp.concatenate([got, got], axis=0))
                    put(blocks + side * RIM + i, value, halo[log_turn, side, i][3:4], False)
                    if turn == 2:
                        put_flags(blocks + side * RIM + i, got[3:4])
            return carry

        lax.fori_loop(0, RIM // 4, some, 0)

    def put_flags(spot, flags):
        flagged[spot] = jnp.where(
            lax.broadcasted_iota(jnp.int32, (16, 128), 0) == 0, flags, F32(1.0)
        ).astype(BF16)

    def exponents(picks, b):
        ahead = jnp.concatenate([far[n] for n in picks], axis=1)
        return dot_left(ahead, own[b])

    def sums(columns, picks, b, exps):
        values = jnp.exp(exps)
        weights = jnp.concatenate([columns(n) for n in picks], axis=1)
        high = values.astype(BF16)
        low = (values - high.astype(F32)).astype(BF16)
        return dot(weights, high) + dot(weights, low)

    def all_sums(one, picked):
        exps = [exponents(picks, b) for picks, b in picked]
        return [one(picks, b, y) for (picks, b), y in zip(picked, exps)]

    def force_columns(n):
        return far[n, :32, :]

    def force_sums(picks, b, exps):
        found = sums(force_columns, picks, b, exps)
        return found[0:8] + found[8:16] + found[16:24]

    def self_pass(amount, one):
        def some(t, carry):
            found = all_sums(one, [([t * amount + u], t * amount + u) for u in range(amount)])
            for u in range(amount):
                acc[t * amount + u] = found[u]
            return carry

        lax.fori_loop(0, blocks // amount, some, 0)

    def move(b, found):
        value = feat8[b]
        found = found * pltpu.roll(value, 4, 0)
        found = found - pltpu.roll(found, 4, 0)
        vel = vel8[b] + slope * one_row(3, b) * found
        pos = pos8[b] + F32(STEP) * vel
        return pos, vel

    def picks_of(b):
        return [pick[b * NB + k] for k in range(1, NB)]

    def force_pass(turn):
        def rim(t, carry):
            spots = [t * 8 + u for u in range(8)] + [blocks - RIM + t * 8 + u for u in range(8)]
            found = all_sums(force_sums, [(picks_of(b), b) for b in spots])
            for u, b in enumerate(spots):
                pos, vel = move(b, found[u] + acc[b])
                keep(turn, b, pos, vel)
                put_stage(turn + 1, u // 8, t * 8 + u % 8, pos, one_row(1 + turn, b))
            return carry

        lax.fori_loop(0, RIM // 8, rim, 0)
        send_halo(turn + 1)

        def inner(t, carry):
            spots = [RIM + t * 16 + u for u in range(16)]
            found = all_sums(force_sums, [(picks_of(b), b) for b in spots])
            for u, b in enumerate(spots):
                pos, vel = move(b, found[u] + acc[b])
                keep(turn, b, pos, vel)
            return carry

        lax.fori_loop(0, (blocks - 2 * RIM) // 16, inner, 0)

    def keep(turn, b, pos, vel):
        pos8[b] = pos
        if turn == 0:
            vel8[b] = vel
        else:
            state[pl.ds(b, 3, stride=blocks), :] = pos[:3]
            state[pl.ds(3 * blocks + b, 3, stride=blocks), :] = vel[:3]

    def state_copy(side):
        return pltpu.make_async_remote_copy(
            src_ref=state,
            dst_ref=swapped.at[side],
            send_sem=state_send.at[side],
            recv_sem=state_recv.at[side],
            device_id=above if side == 0 else below,
            device_id_type=MESH,
        )

    def finish_halo(turn):
        for side in range(2):
            halo_copy(turn, side).wait()

    for turn in range(2):
        own_features(0)
        self_pass(24, force_sums)
        finish_halo(turn)
        halo_features(turn)
        force_pass(turn)

    def start_pair(copy):
        pl.when(has_above)(lambda: copy(0).start())
        pl.when(has_below)(lambda: copy(1).start())

    def wait_pair(copy):
        @pl.when(has_above)
        def _():
            copy(0).wait_send()
            copy(1).wait_recv()

        @pl.when(has_below)
        def _():
            copy(1).wait_send()
            copy(0).wait_recv()

    start_pair(state_copy)

    own_features(1)

    def own_flags(b, carry):
        put_flags(b, one_row(2, b))
        return carry

    lax.fori_loop(0, blocks, own_flags, 0)
    flagged[wide] = jnp.zeros((16, 128), BF16)

    def energy_columns(n):
        return flagged[n]

    def energy_sums(picks, b, exps):
        return sums(energy_columns, picks, b, exps)[:8]

    self_pass(24, energy_sums)
    finish_halo(2)
    halo_features(2)

    def energies(t, carry):
        spots = [t * 16 + u for u in range(16)]
        found = all_sums(energy_sums, [(picks_of(b), b) for b in spots])
        inside_sum, mixed_sum = carry
        for u, b in enumerate(spots):
            both = found[u] + acc[b]
            inside = both[0:1]
            every = both[1:2]
            flags = one_row(2, b)
            plain = strength[pl.ds(b, 1), :]
            inside_sum = inside_sum + plain * flags * inside
            mixed_sum = mixed_sum + plain * (
                flags * (every - inside) + (F32(1.0) - flags) * inside
            )
        return inside_sum, mixed_sum

    blank = jnp.zeros((1, 128), F32)
    inside_sum, mixed_sum = lax.fori_loop(0, blocks // 16, energies, (blank, blank))
    mine = jnp.where(row == 0, inside_sum, jnp.where(row == 1, mixed_sum, level))
    energy[2, here] = mine

    def energy_copy(kind, other, slot):
        line = above if kind == 0 else below if kind == 1 else {}
        return pltpu.make_async_remote_copy(
            src_ref=energy.at[2, here],
            dst_ref=energy.at[kind, slot],
            send_sem=energy_send.at[kind, other],
            recv_sem=energy_recv.at[kind, slot],
            device_id=mate_slab(line, other),
            device_id_type=MESH,
        )

    def send_energy(kind, start):
        for other in range(start, n_slab):
            energy_copy(kind, other, here).start()

    def receive_energy(kind, start):
        for other in range(start, n_slab):
            energy_copy(kind, other, lax.rem(here + other, n_slab)).wait_recv()

    def sent_energy(kind, start):
        for other in range(start, n_slab):
            energy_copy(kind, other, here).wait_send()

    pl.when(has_above)(lambda: send_energy(0, 0))
    pl.when(has_below)(lambda: send_energy(1, 0))
    send_energy(2, 1)

    mate = partner[0]
    taken = accept[0] == 1
    from_below = jnp.full((8, 128), jnp.where(taken & (mate == rep - 1), 1, 0)) == 1
    from_above = jnp.full((8, 128), jnp.where(taken & (mate == rep + 1), 1, 0)) == 1
    wait_pair(state_copy)
    for kind, result in ((0, new_pos), (1, new_vel)):

        def choose(t, carry):
            at = pl.ds(pl.multiple_of(t * 8, 8), 8)
            held = pl.ds(pl.multiple_of(3 * kind * blocks + t * 8, 8), 8)
            value = jnp.where(from_below, swapped[0, held, :], state[held, :])
            result[at, :] = jnp.where(from_above, swapped[1, held, :], value)
            return carry

        lax.fori_loop(0, 3 * blocks // 8, choose, 0)

    pl.when(has_above)(lambda: sent_energy(0, 0))
    pl.when(has_below)(lambda: sent_energy(1, 0))
    sent_energy(2, 1)
    receive_energy(2, 1)
    pl.when(has_below)(lambda: receive_energy(0, 0))
    pl.when(has_above)(lambda: receive_energy(1, 0))

    def whole(kind):
        every = energy[kind, 0]
        for slot in range(1, n_slab):
            every = every + energy[kind, slot]
        every = 0.5 * jnp.sum(every, axis=1, keepdims=True)
        return jnp.where(row == 2, energy[kind, 0], jnp.broadcast_to(every, (8, 128)))

    every = whole(2)
    is_below = jnp.full((8, 128), jnp.where(mate == rep - 1, 1, 0)) == 1
    is_above = jnp.full((8, 128), jnp.where(mate == rep + 1, 1, 0)) == 1
    theirs = jnp.where(is_below, whole(0), jnp.where(is_above, whole(1), every))
    gap = every - theirs
    far_level = theirs[2:3]
    near_level = every[2:3]
    answer = (far_level - near_level) * gap[0:1] + (
        jnp.sqrt(far_level) - jnp.sqrt(near_level)
    ) * gap[1:2]
    answer = answer / F32(total * 128)
    exponent[...] = jnp.broadcast_to(answer, (8, 128))


def hand_over(pos, vel, tile, new_pos, new_vel, exponent):
    new_pos[...] = pos[...]
    new_vel[...] = vel[...]
    exponent[...] = tile[0:1, 0:1]


def shards(
    positions, velocities, strength, inv_mass, solute, scales, neighbours, counts, partner, accept
):
    n_rep = lax.axis_size("rep")
    n_slab = lax.axis_size("slab")
    atoms = positions.shape[2]
    blocks = atoms // 128
    wide = blocks + 2 * RIM
    pairs = 3 * blocks * NB * 128 * 128
    smem = pl.BlockSpec(memory_space=pltpu.SMEM)
    vmem = pl.BlockSpec(memory_space=pltpu.VMEM)
    far = pl.BlockSpec(memory_space=pltpu.HBM)
    rowed = (blocks, 128)
    new_pos, new_vel, exponent = pl.pallas_call(
        functools.partial(kernel, n_rep, n_slab, blocks),
        out_shape=(
            jax.ShapeDtypeStruct((3 * blocks, 128), F32),
            jax.ShapeDtypeStruct((3 * blocks, 128), F32),
            jax.ShapeDtypeStruct((8, 128), F32),
        ),
        in_specs=[pl.BlockSpec(memory_space=pltpu.HBM)] * 10,
        out_specs=(vmem, vmem, vmem),
        scratch_shapes=[
            pltpu.SMEM((1,), F32),
            pltpu.SMEM((NB, blocks), jnp.int32),
            pltpu.SMEM((blocks,), jnp.int32),
            pltpu.SMEM((1,), jnp.int32),
            pltpu.SMEM((1,), jnp.int32),
            pltpu.VMEM((3 * blocks, 128), F32),
            pltpu.VMEM((3 * blocks, 128), F32),
            pltpu.VMEM(rowed, F32),
            pltpu.VMEM(rowed, F32),
            pltpu.VMEM(rowed, jnp.int32),
            pltpu.SemaphoreType.DMA((10,)),
            pltpu.SMEM((blocks * NB,), jnp.int32),
            pltpu.VMEM((blocks, 8, 128), F32),
            pltpu.VMEM((blocks, 8, 128), F32),
            pltpu.VMEM((blocks, 8, 128), F32),
            pltpu.VMEM((blocks, 48, 128), BF16),
            pltpu.VMEM((wide + 1, 48, 128), BF16),
            pltpu.VMEM((wide + 1, 16, 128), BF16),
            pltpu.VMEM((blocks, 8, 128), F32),
            pltpu.VMEM((4, blocks, 128), F32),
            pltpu.VMEM((3, 2, RIM, 4, 128), F32),
            pltpu.VMEM((3, 2, RIM, 4, 128), F32),
            pltpu.VMEM((6 * blocks, 128), F32),
            pltpu.VMEM((2, 6 * blocks, 128), F32),
            pltpu.VMEM((3, n_slab, 8, 128), F32),
            pltpu.SemaphoreType.DMA((3, 2)),
            pltpu.SemaphoreType.DMA((3, 2)),
            pltpu.SemaphoreType.DMA((2,)),
            pltpu.SemaphoreType.DMA((2,)),
            pltpu.SemaphoreType.DMA((3, n_slab)),
            pltpu.SemaphoreType.DMA((3, n_slab)),
        ],
        compiler_params=pltpu.CompilerParams(
            collective_id=0, has_side_effects=True, vmem_limit_bytes=56 << 20
        ),
        cost_estimate=pl.CostEstimate(
            flops=pairs * 100, bytes_accessed=1 << 20, transcendentals=pairs
        ),
    )(
        scales,
        neighbours.T,
        counts,
        partner,
        accept,
        positions.reshape(3 * blocks, 128),
        velocities.reshape(3 * blocks, 128),
        strength.reshape(rowed),
        inv_mass.reshape(rowed),
        solute.reshape(rowed),
    )
    shape = positions.shape
    new_pos, new_vel, exponent = pl.pallas_call(
        hand_over,
        out_shape=(
            jax.ShapeDtypeStruct((3 * blocks, 128), F32),
            jax.ShapeDtypeStruct((3 * blocks, 128), F32),
            jax.ShapeDtypeStruct((1, 1), F32),
        ),
        in_specs=[vmem, vmem, vmem],
        out_specs=(vmem, vmem, vmem),
    )(new_pos, new_vel, exponent)
    return (new_pos.reshape(shape), new_vel.reshape(shape), exponent.reshape(1))


def solution(mesh):
    placed = (
        P("rep", None, "slab"),
        P("rep", None, "slab"),
        P("slab"),
        P("slab"),
        P("slab"),
        P("rep"),
        P("slab", None),
        P("slab"),
        P("rep"),
        P("rep"),
    )
    return jax.shard_map(
        shards,
        mesh=mesh,
        in_specs=placed,
        out_specs=(P("rep", None, "slab"), P("rep", None, "slab"), P("rep")),
        check_vma=False,
    )
```

```python
import functools
import math

import jax
import jax.numpy as jnp
from jax import lax
from jax.experimental import pallas as pl
from jax.experimental.pallas import tpu as pltpu
from jax.sharding import PartitionSpec as P

NB = 4
RIM = 16
SIGMA = 0.35
BOX = 2.0
STEP = 0.02
NONE = -1000.0
MESH = pl.DeviceIdType.MESH
F32 = jnp.float32
BF16 = jnp.bfloat16
SINE = (
    6.28318530717,
    -41.34170211,
    81.60522621,
    -76.70428132,
    42.00980576,
    -14.39413556,
)


def dot(a, b):
    return jnp.dot(a, b, preferred_element_type=F32)


def dot_left(a, b):
    return lax.dot_general(a, b, (((0,), (0,)), ((), ())), preferred_element_type=F32)


def parts(value):
    first = value.astype(BF16).astype(F32)
    rest = value - first
    second = rest.astype(BF16).astype(F32)
    third = rest - second
    return first, second, third


def kernel(
    n_rep,
    n_slab,
    blocks,
    scales_far,
    listed_far,
    counts_far,
    partner_far,
    accept_far,
    positions_far,
    velocities_far,
    strength_far,
    inv_mass_far,
    solute_far,
    new_pos,
    new_vel,
    exponent,
    scales,
    listed,
    counts,
    partner,
    accept,
    positions,
    velocities,
    strength,
    inv_mass,
    solute,
    fetch,
    pick,
    pos8,
    vel8,
    feat8,
    own,
    far,
    flagged,
    acc,
    rows,
    stage,
    halo,
    state,
    swapped,
    energy,
    halo_send,
    halo_recv,
    state_send,
    state_recv,
    energy_send,
    energy_recv,
):
    rep = lax.axis_index("rep")
    here = lax.axis_index("slab")
    above = {"rep": jnp.minimum(rep + 1, n_rep - 1)}
    below = {"rep": jnp.maximum(rep - 1, 0)}
    after = {"slab": lax.rem(here + 1, n_slab)}
    before = {"slab": lax.rem(here + n_slab - 1, n_slab)}
    wide = blocks + 2 * RIM

    fetches = [
        pltpu.make_async_copy(source, target, fetch.at[i])
        for i, (source, target) in enumerate(
            (
                (strength_far, strength),
                (solute_far, solute),
                (inv_mass_far, inv_mass),
                (scales_far, scales),
                (positions_far, positions),
                (velocities_far, velocities),
                (listed_far, listed),
                (counts_far, counts),
                (partner_far, partner),
                (accept_far, accept),
            )
        )
    ]
    for copy in fetches:
        copy.start()
    barrier = pltpu.get_barrier_semaphore()
    has_below = rep > 0
    has_above = rep < n_rep - 1

    def mate_slab(line, other):
        return {**line, "slab": lax.rem(here + other, n_slab)}

    def greet(line, start):
        for other in range(start, n_slab):
            pl.semaphore_signal(
                barrier, 1, device_id=mate_slab(line, other), device_id_type=MESH
            )

    greet({}, 1)
    pl.when(has_below)(lambda: greet(below, 0))
    pl.when(has_above)(lambda: greet(above, 0))

    row = lax.broadcasted_iota(jnp.int32, (8, 128), 0)
    long = (row == 0) | (row == 4)
    is3 = row == 3
    is7 = row == 7
    periods = (float(n_slab), BOX)
    inverse = jnp.where(long, F32(1.0 / periods[0]), F32(1.0 / periods[1]))
    phase = jnp.where(row >= 4, F32(0.25), F32(0.0))
    heights = [p * p / (2.0 * math.pi**2) / (2.0 * SIGMA**2) for p in periods]
    height = jnp.where(long, F32(math.sqrt(heights[0])), F32(math.sqrt(heights[1])))
    shift = heights[0] + 2.0 * heights[1]
    slope = [STEP * p / math.pi / (2.0 * SIGMA**2) / h for p, h in zip(periods, heights)]
    slope = jnp.where(long, F32(slope[0]), F32(slope[1]))
    slope = jnp.where(is3 | is7, F32(0.0), jnp.where(row >= 4, -slope, slope))

    def features(x):
        turn = x * inverse - phase
        turn = turn - jnp.floor(turn + 0.5)
        w = 0.25 - jnp.abs(turn)
        z = w * w
        value = F32(SINE[-1])
        for c in SINE[-2::-1]:
            value = value * z + F32(c)
        return value * (w * height)

    fixed = parts(jnp.where(is3, F32(-shift), F32(1.0)))

    def put(spot, value, log_weight, owned):
        value = jnp.where(is3, F32(1.0), jnp.where(is7, log_weight, value))
        a, b, c = parts(value)
        far[spot] = jnp.concatenate([a, b, c, a, b, a], axis=0).astype(BF16)
        if owned:
            x, y, z = [jnp.where(is3 | is7, k, v) for k, v in zip(fixed, (a, b, c))]
            own[spot] = jnp.concatenate([x, x, x, y, y, z], axis=0).astype(BF16)

    for copy in fetches:
        copy.wait()

    level = jnp.full((8, 128), scales[0], F32)
    root = jnp.sqrt(level)

    def atom_rows(t, carry):
        at = pl.ds(pl.multiple_of(t * 8, 8), 8)
        plain = strength[at, :]
        chosen = solute[at, :] == 1
        scaled = plain * jnp.where(chosen, root, F32(1.0))
        rows[0, at, :] = jnp.log(scaled)
        rows[1, at, :] = jnp.log(plain)
        rows[2, at, :] = jnp.where(chosen, F32(1.0), F32(0.0))
        rows[3, at, :] = scaled * inv_mass[at, :]
        return carry

    lax.fori_loop(0, blocks // 8, atom_rows, 0)

    def one_row(which, b):
        return rows[which, pl.ds(b, 1), :]

    def put_stage(turn, side, i, x, extra):
        stage[turn, side, i] = jnp.where(is3, extra, x)[:4]

    def load(b):
        blank = jnp.zeros((1, 128), F32)
        x = positions[pl.ds(b, 3, stride=blocks), :]
        v = velocities[pl.ds(b, 3, stride=blocks), :]
        pos8[b] = jnp.concatenate([x, blank, x, blank], axis=0)
        vel8[b] = jnp.concatenate([v, blank, v, blank], axis=0)

    def load_some(t, carry):
        for u in range(4):
            load(t * 4 + u)
        return carry

    lax.fori_loop(0, blocks // 4, load_some, 0)

    def stage_first(i, carry):
        low = i
        high = blocks - RIM + i
        put_stage(0, 0, i, pos8[low], one_row(0, low))
        put_stage(0, 1, i, pos8[high], one_row(0, high))
        return carry

    lax.fori_loop(0, RIM, stage_first, 0)
    lines = has_below.astype(jnp.int32) + has_above.astype(jnp.int32)
    pl.semaphore_wait(barrier, n_slab - 1 + n_slab * lines)

    def halo_copy(turn, side):
        return pltpu.make_async_remote_copy(
            src_ref=stage.at[turn, side],
            dst_ref=halo.at[turn, side],
            send_sem=halo_send.at[turn, side],
            recv_sem=halo_recv.at[turn, side],
            device_id=before if side == 0 else after,
            device_id_type=MESH,
        )

    def send_halo(turn):
        for side in range(2):
            halo_copy(turn, side).start()

    send_halo(0)

    first = here * blocks
    total = n_slab * blocks

    def find(b, carry):
        count = counts[b]
        for k in range(1, NB):
            near = listed[k, b] - first
            near = jnp.where(near < 0, near + total, near)
            near = jnp.where(near < blocks + RIM, near, near - (total - blocks - 2 * RIM))
            pick[b * NB + k] = jnp.where(k < count, near, wide)
        return carry

    lax.fori_loop(0, blocks, find, 0)

    far[wide] = jnp.concatenate(
        [jnp.where(is7, F32(NONE), F32(0.0)), jnp.zeros((40, 128), F32)], axis=0
    ).astype(BF16)

    def own_features(which):
        def some(t, carry):
            for u in range(12):
                b = t * 12 + u
                value = features(pos8[b])
                feat8[b] = value
                put(b, value, one_row(which, b), True)
            return carry

        lax.fori_loop(0, blocks // 12, some, 0)

    def halo_features(turn):
        log_turn = 1 if turn == 2 else 0

        def some(t, carry):
            for side in range(2):
                for u in range(4):
                    i = t * 4 + u
                    got = halo[turn, side, i]
                    value = features(jnp.concatenate([got, got], axis=0))
                    put(blocks + side * RIM + i, value, halo[log_turn, side, i][3:4], False)
                    if turn == 2:
                        put_flags(blocks + side * RIM + i, got[3:4])
            return carry

        lax.fori_loop(0, RIM // 4, some, 0)

    def put_flags(spot, flags):
        flagged[spot] = jnp.where(
            lax.broadcasted_iota(jnp.int32, (16, 128), 0) == 0, flags, F32(1.0)
        ).astype(BF16)

    def exponents(picks, b):
        ahead = jnp.concatenate([far[n] for n in picks], axis=1)
        return dot_left(ahead, own[b])

    def sums(columns, picks, b, exps):
        values = jnp.exp(exps)
        weights = jnp.concatenate([columns(n) for n in picks], axis=1)
        high = values.astype(BF16)
        low = (values - high.astype(F32)).astype(BF16)
        return dot(weights, high) + dot(weights, low)

    def all_sums(one, picked):
        exps = [exponents(picks, b) for picks, b in picked]
        return [one(picks, b, y) for (picks, b), y in zip(picked, exps)]

    def force_columns(n):
        return far[n, :32, :]

    def force_sums(picks, b, exps):
        found = sums(force_columns, picks, b, exps)
        return found[0:8] + found[8:16] + found[16:24]

    def self_pass(amount, one):
        def some(t, carry):
            found = all_sums(one, [([t * amount + u], t * amount + u) for u in range(amount)])
            for u in range(amount):
                acc[t * amount + u] = found[u]
            return carry

        lax.fori_loop(0, blocks // amount, some, 0)

    def move(b, found):
        value = feat8[b]
        found = found * pltpu.roll(value, 4, 0)
        found = found - pltpu.roll(found, 4, 0)
        vel = vel8[b] + slope * one_row(3, b) * found
        pos = pos8[b] + F32(STEP) * vel
        return pos, vel

    def picks_of(b):
        return [pick[b * NB + k] for k in range(1, NB)]

    def force_pass(turn):
        def rim(t, carry):
            spots = [t * 8 + u for u in range(8)] + [blocks - RIM + t * 8 + u for u in range(8)]
            found = all_sums(force_sums, [(picks_of(b), b) for b in spots])
            for u, b in enumerate(spots):
                pos, vel = move(b, found[u] + acc[b])
                keep(turn, b, pos, vel)
                put_stage(turn + 1, u // 8, t * 8 + u % 8, pos, one_row(1 + turn, b))
            return carry

        lax.fori_loop(0, RIM // 8, rim, 0)
        send_halo(turn + 1)

        def inner(t, carry):
            spots = [RIM + t * 16 + u for u in range(16)]
            found = all_sums(force_sums, [(picks_of(b), b) for b in spots])
            for u, b in enumerate(spots):
                pos, vel = move(b, found[u] + acc[b])
                keep(turn, b, pos, vel)
            return carry

        lax.fori_loop(0, (blocks - 2 * RIM) // 16, inner, 0)

    def keep(turn, b, pos, vel):
        pos8[b] = pos
        if turn == 0:
            vel8[b] = vel
        else:
            state[pl.ds(b, 3, stride=blocks), :] = pos[:3]
            state[pl.ds(3 * blocks + b, 3, stride=blocks), :] = vel[:3]

    def state_copy(side):
        return pltpu.make_async_remote_copy(
            src_ref=state,
            dst_ref=swapped.at[side],
            send_sem=state_send.at[side],
            recv_sem=state_recv.at[side],
            device_id=above if side == 0 else below,
            device_id_type=MESH,
        )

    def finish_halo(turn):
        for side in range(2):
            halo_copy(turn, side).wait()

    for turn in range(2):
        own_features(0)
        self_pass(48, force_sums)
        finish_halo(turn)
        halo_features(turn)
        force_pass(turn)

    def start_pair(copy):
        pl.when(has_above)(lambda: copy(0).start())
        pl.when(has_below)(lambda: copy(1).start())

    def wait_pair(copy):
        @pl.when(has_above)
        def _():
            copy(0).wait_send()
            copy(1).wait_recv()

        @pl.when(has_below)
        def _():
            copy(1).wait_send()
            copy(0).wait_recv()

    start_pair(state_copy)

    own_features(1)

    def own_flags(b, carry):
        put_flags(b, one_row(2, b))
        return carry

    lax.fori_loop(0, blocks, own_flags, 0)
    flagged[wide] = jnp.zeros((16, 128), BF16)

    def energy_columns(n):
        return flagged[n]

    def energy_sums(picks, b, exps):
        return sums(energy_columns, picks, b, exps)[:8]

    self_pass(48, energy_sums)
    finish_halo(2)
    halo_features(2)

    def energies(t, carry):
        spots = [t * 24 + u for u in range(24)]
        found = all_sums(energy_sums, [(picks_of(b), b) for b in spots])
        inside_sum, mixed_sum = carry
        for u, b in enumerate(spots):
            both = found[u] + acc[b]
            inside = both[0:1]
            every = both[1:2]
            flags = one_row(2, b)
            plain = strength[pl.ds(b, 1), :]
            inside_sum = inside_sum + plain * flags * inside
            mixed_sum = mixed_sum + plain * (
                flags * (every - inside) + (F32(1.0) - flags) * inside
            )
        return inside_sum, mixed_sum

    blank = jnp.zeros((1, 128), F32)
    inside_sum, mixed_sum = lax.fori_loop(0, blocks // 24, energies, (blank, blank))
    mine = jnp.where(row == 0, inside_sum, jnp.where(row == 1, mixed_sum, level))
    energy[2, here] = mine

    def energy_copy(kind, other, slot):
        line = above if kind == 0 else below if kind == 1 else {}
        return pltpu.make_async_remote_copy(
            src_ref=energy.at[2, here],
            dst_ref=energy.at[kind, slot],
            send_sem=energy_send.at[kind, other],
            recv_sem=energy_recv.at[kind, slot],
            device_id=mate_slab(line, other),
            device_id_type=MESH,
        )

    def send_energy(kind, start):
        for other in range(start, n_slab):
            energy_copy(kind, other, here).start()

    def receive_energy(kind, start):
        for other in range(start, n_slab):
            energy_copy(kind, other, lax.rem(here + other, n_slab)).wait_recv()

    def sent_energy(kind, start):
        for other in range(start, n_slab):
            energy_copy(kind, other, here).wait_send()

    pl.when(has_above)(lambda: send_energy(0, 0))
    pl.when(has_below)(lambda: send_energy(1, 0))
    send_energy(2, 1)

    mate = partner[0]
    taken = accept[0] == 1
    from_below = jnp.full((8, 128), jnp.where(taken & (mate == rep - 1), 1, 0)) == 1
    from_above = jnp.full((8, 128), jnp.where(taken & (mate == rep + 1), 1, 0)) == 1
    wait_pair(state_copy)
    for kind, result in ((0, new_pos), (1, new_vel)):

        def choose(t, carry):
            at = pl.ds(pl.multiple_of(t * 8, 8), 8)
            held = pl.ds(pl.multiple_of(3 * kind * blocks + t * 8, 8), 8)
            value = jnp.where(from_below, swapped[0, held, :], state[held, :])
            result[at, :] = jnp.where(from_above, swapped[1, held, :], value)
            return carry

        lax.fori_loop(0, 3 * blocks // 8, choose, 0)

    pl.when(has_above)(lambda: sent_energy(0, 0))
    pl.when(has_below)(lambda: sent_energy(1, 0))
    sent_energy(2, 1)
    receive_energy(2, 1)
    pl.when(has_below)(lambda: receive_energy(0, 0))
    pl.when(has_above)(lambda: receive_energy(1, 0))

    def whole(kind):
        every = energy[kind, 0]
        for slot in range(1, n_slab):
            every = every + energy[kind, slot]
        every = 0.5 * jnp.sum(every, axis=1, keepdims=True)
        return jnp.where(row == 2, energy[kind, 0], jnp.broadcast_to(every, (8, 128)))

    every = whole(2)
    is_below = jnp.full((8, 128), jnp.where(mate == rep - 1, 1, 0)) == 1
    is_above = jnp.full((8, 128), jnp.where(mate == rep + 1, 1, 0)) == 1
    theirs = jnp.where(is_below, whole(0), jnp.where(is_above, whole(1), every))
    gap = every - theirs
    far_level = theirs[2:3]
    near_level = every[2:3]
    answer = (far_level - near_level) * gap[0:1] + (
        jnp.sqrt(far_level) - jnp.sqrt(near_level)
    ) * gap[1:2]
    answer = answer / F32(total * 128)
    exponent[...] = jnp.broadcast_to(answer, (8, 128))


def hand_over(pos, vel, tile, new_pos, new_vel, exponent):
    new_pos[...] = pos[...]
    new_vel[...] = vel[...]
    exponent[...] = tile[0:1, 0:1]


def shards(
    positions, velocities, strength, inv_mass, solute, scales, neighbours, counts, partner, accept
):
    n_rep = lax.axis_size("rep")
    n_slab = lax.axis_size("slab")
    atoms = positions.shape[2]
    blocks = atoms // 128
    wide = blocks + 2 * RIM
    pairs = 3 * blocks * NB * 128 * 128
    smem = pl.BlockSpec(memory_space=pltpu.SMEM)
    vmem = pl.BlockSpec(memory_space=pltpu.VMEM)
    far = pl.BlockSpec(memory_space=pltpu.HBM)
    rowed = (blocks, 128)
    new_pos, new_vel, exponent = pl.pallas_call(
        functools.partial(kernel, n_rep, n_slab, blocks),
        out_shape=(
            jax.ShapeDtypeStruct((3 * blocks, 128), F32),
            jax.ShapeDtypeStruct((3 * blocks, 128), F32),
            jax.ShapeDtypeStruct((8, 128), F32),
        ),
        in_specs=[pl.BlockSpec(memory_space=pltpu.HBM)] * 10,
        out_specs=(vmem, vmem, vmem),
        scratch_shapes=[
            pltpu.SMEM((1,), F32),
            pltpu.SMEM((NB, blocks), jnp.int32),
            pltpu.SMEM((blocks,), jnp.int32),
            pltpu.SMEM((1,), jnp.int32),
            pltpu.SMEM((1,), jnp.int32),
            pltpu.VMEM((3 * blocks, 128), F32),
            pltpu.VMEM((3 * blocks, 128), F32),
            pltpu.VMEM(rowed, F32),
            pltpu.VMEM(rowed, F32),
            pltpu.VMEM(rowed, jnp.int32),
            pltpu.SemaphoreType.DMA((10,)),
            pltpu.SMEM((blocks * NB,), jnp.int32),
            pltpu.VMEM((blocks, 8, 128), F32),
            pltpu.VMEM((blocks, 8, 128), F32),
            pltpu.VMEM((blocks, 8, 128), F32),
            pltpu.VMEM((blocks, 48, 128), BF16),
            pltpu.VMEM((wide + 1, 48, 128), BF16),
            pltpu.VMEM((wide + 1, 16, 128), BF16),
            pltpu.VMEM((blocks, 8, 128), F32),
            pltpu.VMEM((4, blocks, 128), F32),
            pltpu.VMEM((3, 2, RIM, 4, 128), F32),
            pltpu.VMEM((3, 2, RIM, 4, 128), F32),
            pltpu.VMEM((6 * blocks, 128), F32),
            pltpu.VMEM((2, 6 * blocks, 128), F32),
            pltpu.VMEM((3, n_slab, 8, 128), F32),
            pltpu.SemaphoreType.DMA((3, 2)),
            pltpu.SemaphoreType.DMA((3, 2)),
            pltpu.SemaphoreType.DMA((2,)),
            pltpu.SemaphoreType.DMA((2,)),
            pltpu.SemaphoreType.DMA((3, n_slab)),
            pltpu.SemaphoreType.DMA((3, n_slab)),
        ],
        compiler_params=pltpu.CompilerParams(
            collective_id=0, has_side_effects=True, vmem_limit_bytes=56 << 20
        ),
        cost_estimate=pl.CostEstimate(
            flops=pairs * 100, bytes_accessed=1 << 20, transcendentals=pairs
        ),
    )(
        scales,
        neighbours.T,
        counts,
        partner,
        accept,
        positions.reshape(3 * blocks, 128),
        velocities.reshape(3 * blocks, 128),
        strength.reshape(rowed),
        inv_mass.reshape(rowed),
        solute.reshape(rowed),
    )
    shape = positions.shape
    new_pos, new_vel, exponent = pl.pallas_call(
        hand_over,
        out_shape=(
            jax.ShapeDtypeStruct((3 * blocks, 128), F32),
            jax.ShapeDtypeStruct((3 * blocks, 128), F32),
            jax.ShapeDtypeStruct((1, 1), F32),
        ),
        in_specs=[vmem, vmem, vmem],
        out_specs=(vmem, vmem, vmem),
    )(new_pos, new_vel, exponent)
    return (new_pos.reshape(shape), new_vel.reshape(shape), exponent.reshape(1))


def solution(mesh):
    placed = (
        P("rep", None, "slab"),
        P("rep", None, "slab"),
        P("slab"),
        P("slab"),
        P("slab"),
        P("rep"),
        P("slab", None),
        P("slab"),
        P("rep"),
        P("rep"),
    )
    return jax.shard_map(
        shards,
        mesh=mesh,
        in_specs=placed,
        out_specs=(P("rep", None, "slab"), P("rep", None, "slab"), P("rep")),
        check_vma=False,
    )
```

```python
import functools
import math

import jax
import jax.numpy as jnp
from jax import lax
from jax.experimental import pallas as pl
from jax.experimental.pallas import tpu as pltpu
from jax.sharding import PartitionSpec as P

NB = 4
RIM = 16
SIGMA = 0.35
BOX = 2.0
STEP = 0.02
NONE = -1000.0
MESH = pl.DeviceIdType.MESH
F32 = jnp.float32
BF16 = jnp.bfloat16
SINE = (
    6.28318530717,
    -41.34170211,
    81.60522621,
    -76.70428132,
    42.00980576,
    -14.39413556,
)


def dot(a, b):
    return jnp.dot(a, b, preferred_element_type=F32)


def dot_left(a, b):
    return lax.dot_general(a, b, (((0,), (0,)), ((), ())), preferred_element_type=F32)


def parts(value):
    first = value.astype(BF16).astype(F32)
    rest = value - first
    second = rest.astype(BF16).astype(F32)
    third = rest - second
    return first, second, third


def kernel(
    n_rep,
    n_slab,
    blocks,
    scales_far,
    listed_far,
    counts_far,
    partner_far,
    accept_far,
    positions_far,
    velocities_far,
    strength_far,
    inv_mass_far,
    solute_far,
    new_pos_far,
    new_vel_far,
    exponent,
    new_pos,
    new_vel,
    leave,
    scales,
    listed,
    counts,
    partner,
    accept,
    positions,
    velocities,
    strength,
    inv_mass,
    solute,
    fetch,
    pick,
    pos8,
    vel8,
    feat8,
    own,
    far,
    flagged,
    acc,
    rows,
    stage,
    halo,
    state,
    swapped,
    energy,
    halo_send,
    halo_recv,
    state_send,
    state_recv,
    energy_send,
    energy_recv,
):
    rep = lax.axis_index("rep")
    here = lax.axis_index("slab")
    above = {"rep": jnp.minimum(rep + 1, n_rep - 1)}
    below = {"rep": jnp.maximum(rep - 1, 0)}
    after = {"slab": lax.rem(here + 1, n_slab)}
    before = {"slab": lax.rem(here + n_slab - 1, n_slab)}
    wide = blocks + 2 * RIM

    fetches = [
        pltpu.make_async_copy(source, target, fetch.at[i])
        for i, (source, target) in enumerate(
            (
                (strength_far, strength),
                (solute_far, solute),
                (inv_mass_far, inv_mass),
                (scales_far, scales),
                (positions_far, positions),
                (velocities_far, velocities),
                (listed_far, listed),
                (counts_far, counts),
                (partner_far, partner),
                (accept_far, accept),
            )
        )
    ]
    for copy in fetches:
        copy.start()
    barrier = pltpu.get_barrier_semaphore()
    has_below = rep > 0
    has_above = rep < n_rep - 1

    def mate_slab(line, other):
        return {**line, "slab": lax.rem(here + other, n_slab)}

    def greet(line, start):
        for other in range(start, n_slab):
            pl.semaphore_signal(
                barrier, 1, device_id=mate_slab(line, other), device_id_type=MESH
            )

    greet({}, 1)
    pl.when(has_below)(lambda: greet(below, 0))
    pl.when(has_above)(lambda: greet(above, 0))

    row = lax.broadcasted_iota(jnp.int32, (8, 128), 0)
    long = (row == 0) | (row == 4)
    is3 = row == 3
    is7 = row == 7
    periods = (float(n_slab), BOX)
    inverse = jnp.where(long, F32(1.0 / periods[0]), F32(1.0 / periods[1]))
    phase = jnp.where(row >= 4, F32(0.25), F32(0.0))
    heights = [p * p / (2.0 * math.pi**2) / (2.0 * SIGMA**2) for p in periods]
    height = jnp.where(long, F32(math.sqrt(heights[0])), F32(math.sqrt(heights[1])))
    shift = heights[0] + 2.0 * heights[1]
    slope = [STEP * p / math.pi / (2.0 * SIGMA**2) / h for p, h in zip(periods, heights)]
    slope = jnp.where(long, F32(slope[0]), F32(slope[1]))
    slope = jnp.where(is3 | is7, F32(0.0), jnp.where(row >= 4, -slope, slope))

    def features(x):
        turn = x * inverse - phase
        turn = turn - jnp.floor(turn + 0.5)
        w = 0.25 - jnp.abs(turn)
        z = w * w
        value = F32(SINE[-1])
        for c in SINE[-2::-1]:
            value = value * z + F32(c)
        return value * (w * height)

    fixed = parts(jnp.where(is3, F32(-shift), F32(1.0)))

    def put(spot, value, log_weight, owned):
        value = jnp.where(is3, F32(1.0), jnp.where(is7, log_weight, value))
        a, b, c = parts(value)
        far[spot] = jnp.concatenate([a, b, c, a, b, a], axis=0).astype(BF16)
        if owned:
            x, y, z = [jnp.where(is3 | is7, k, v) for k, v in zip(fixed, (a, b, c))]
            own[spot] = jnp.concatenate([x, x, x, y, y, z], axis=0).astype(BF16)

    for copy in fetches[:5]:
        copy.wait()

    level = jnp.full((8, 128), scales[0], F32)
    root = jnp.sqrt(level)

    plain = strength[...]
    chosen = solute[...] == 1
    scaled = plain * jnp.where(chosen, root[0:1], F32(1.0))
    rows[0] = jnp.log(scaled)
    rows[1] = jnp.log(plain)
    rows[2] = jnp.where(chosen, F32(1.0), F32(0.0))
    rows[3] = scaled * inv_mass[...]

    def one_row(which, b):
        return rows[which, pl.ds(b, 1), :]

    def put_stage(turn, side, i, x, extra):
        stage[turn, side, i] = jnp.where(is3, extra, x)[:4]

    def stage_first(t, carry):
        for u in range(4):
            i = t * 4 + u
            for side, b in ((0, i), (1, blocks - RIM + i)):
                x = positions[pl.ds(b, 3, stride=blocks), :]
                stage[0, side, i] = jnp.concatenate([x, one_row(0, b)], axis=0)
        return carry

    lax.fori_loop(0, RIM // 4, stage_first, 0)
    lines = has_below.astype(jnp.int32) + has_above.astype(jnp.int32)
    pl.semaphore_wait(barrier, n_slab - 1 + n_slab * lines)

    def halo_copy(turn, side):
        return pltpu.make_async_remote_copy(
            src_ref=stage.at[turn, side],
            dst_ref=halo.at[turn, side],
            send_sem=halo_send.at[turn, side],
            recv_sem=halo_recv.at[turn, side],
            device_id=before if side == 0 else after,
            device_id_type=MESH,
        )

    def send_halo(turn):
        for side in range(2):
            halo_copy(turn, side).start()

    send_halo(0)
    for copy in fetches[5:]:
        copy.wait()

    def load(b):
        blank = jnp.zeros((1, 128), F32)
        x = positions[pl.ds(b, 3, stride=blocks), :]
        v = velocities[pl.ds(b, 3, stride=blocks), :]
        pos8[b] = jnp.concatenate([x, blank, x, blank], axis=0)
        vel8[b] = jnp.concatenate([v, blank, v, blank], axis=0)

    def load_some(t, carry):
        for u in range(4):
            load(t * 4 + u)
        return carry

    lax.fori_loop(0, blocks // 4, load_some, 0)

    first = here * blocks
    total = n_slab * blocks

    def find(b, carry):
        count = counts[b]
        for k in range(1, NB):
            near = listed[k, b] - first
            near = jnp.where(near < 0, near + total, near)
            near = jnp.where(near < blocks + RIM, near, near - (total - blocks - 2 * RIM))
            pick[b * NB + k] = jnp.where(k < count, near, wide)
        return carry

    lax.fori_loop(0, blocks, find, 0)

    far[wide] = jnp.concatenate(
        [jnp.where(is7, F32(NONE), F32(0.0)), jnp.zeros((40, 128), F32)], axis=0
    ).astype(BF16)

    def own_features(which):
        def some(t, carry):
            for u in range(12):
                b = t * 12 + u
                value = features(pos8[b])
                feat8[b] = value
                put(b, value, one_row(which, b), True)
            return carry

        lax.fori_loop(0, blocks // 12, some, 0)

    def halo_features(turn):
        log_turn = 1 if turn == 2 else 0

        def some(t, carry):
            for side in range(2):
                for u in range(4):
                    i = t * 4 + u
                    got = halo[turn, side, i]
                    value = features(jnp.concatenate([got, got], axis=0))
                    put(blocks + side * RIM + i, value, halo[log_turn, side, i][3:4], False)
                    if turn == 2:
                        put_flags(blocks + side * RIM + i, got[3:4])
            return carry

        lax.fori_loop(0, RIM // 4, some, 0)

    def put_flags(spot, flags):
        flagged[spot] = jnp.where(
            lax.broadcasted_iota(jnp.int32, (16, 128), 0) == 0, flags, F32(1.0)
        ).astype(BF16)

    def exponents(picks, b):
        ahead = jnp.concatenate([far[n] for n in picks], axis=1)
        return dot_left(ahead, own[b])

    def sums(columns, picks, b, exps):
        values = jnp.exp(exps)
        weights = jnp.concatenate([columns(n) for n in picks], axis=1)
        high = values.astype(BF16)
        low = (values - high.astype(F32)).astype(BF16)
        return dot(weights, high) + dot(weights, low)

    def all_sums(one, picked):
        exps = [exponents(picks, b) for picks, b in picked]
        return [one(picks, b, y) for (picks, b), y in zip(picked, exps)]

    def force_columns(n):
        return far[n, :32, :]

    def force_sums(picks, b, exps):
        found = sums(force_columns, picks, b, exps)
        return found[0:8] + found[8:16] + found[16:24]

    def self_pass(amount, one):
        def some(t, carry):
            found = all_sums(one, [([t * amount + u], t * amount + u) for u in range(amount)])
            for u in range(amount):
                acc[t * amount + u] = found[u]
            return carry

        lax.fori_loop(0, blocks // amount, some, 0)

    def move(b, found):
        value = feat8[b]
        found = found * pltpu.roll(value, 4, 0)
        found = found - pltpu.roll(found, 4, 0)
        vel = vel8[b] + slope * one_row(3, b) * found
        pos = pos8[b] + F32(STEP) * vel
        return pos, vel

    def picks_of(b):
        return [pick[b * NB + k] for k in range(1, NB)]

    def force_pass(turn):
        def rim(t, carry):
            spots = [t * 8 + u for u in range(8)] + [blocks - RIM + t * 8 + u for u in range(8)]
            found = all_sums(force_sums, [(picks_of(b), b) for b in spots])
            for u, b in enumerate(spots):
                pos, vel = move(b, found[u] + acc[b])
                keep(turn, b, pos, vel)
                put_stage(turn + 1, u // 8, t * 8 + u % 8, pos, one_row(1 + turn, b))
            return carry

        lax.fori_loop(0, RIM // 8, rim, 0)
        send_halo(turn + 1)

        def inner(t, carry):
            spots = [RIM + t * 16 + u for u in range(16)]
            found = all_sums(force_sums, [(picks_of(b), b) for b in spots])
            for u, b in enumerate(spots):
                pos, vel = move(b, found[u] + acc[b])
                keep(turn, b, pos, vel)
            return carry

        lax.fori_loop(0, (blocks - 2 * RIM) // 16, inner, 0)

    def keep(turn, b, pos, vel):
        pos8[b] = pos
        if turn == 0:
            vel8[b] = vel
        else:
            state[pl.ds(b, 3, stride=blocks), :] = pos[:3]
            state[pl.ds(3 * blocks + b, 3, stride=blocks), :] = vel[:3]

    def state_copy(side):
        return pltpu.make_async_remote_copy(
            src_ref=state,
            dst_ref=swapped.at[side],
            send_sem=state_send.at[side],
            recv_sem=state_recv.at[side],
            device_id=above if side == 0 else below,
            device_id_type=MESH,
        )

    def finish_halo(turn):
        for side in range(2):
            halo_copy(turn, side).wait()

    for turn in range(2):
        own_features(0)
        self_pass(24, force_sums)
        finish_halo(turn)
        halo_features(turn)
        force_pass(turn)

    def start_pair(copy):
        pl.when(has_above)(lambda: copy(0).start())
        pl.when(has_below)(lambda: copy(1).start())

    def wait_pair(copy):
        @pl.when(has_above)
        def _():
            copy(0).wait_send()
            copy(1).wait_recv()

        @pl.when(has_below)
        def _():
            copy(1).wait_send()
            copy(0).wait_recv()

    start_pair(state_copy)

    own_features(1)

    def own_flags(b, carry):
        put_flags(b, one_row(2, b))
        return carry

    lax.fori_loop(0, blocks, own_flags, 0)
    flagged[wide] = jnp.zeros((16, 128), BF16)

    def energy_columns(n):
        return flagged[n]

    def energy_sums(picks, b, exps):
        return sums(energy_columns, picks, b, exps)[:8]

    self_pass(24, energy_sums)
    finish_halo(2)
    halo_features(2)

    def energies(t, carry):
        spots = [t * 16 + u for u in range(16)]
        found = all_sums(energy_sums, [(picks_of(b), b) for b in spots])
        inside_sum, mixed_sum = carry
        for u, b in enumerate(spots):
            both = found[u] + acc[b]
            inside = both[0:1]
            every = both[1:2]
            flags = one_row(2, b)
            plain = strength[pl.ds(b, 1), :]
            inside_sum = inside_sum + plain * flags * inside
            mixed_sum = mixed_sum + plain * (
                flags * (every - inside) + (F32(1.0) - flags) * inside
            )
        return inside_sum, mixed_sum

    blank = jnp.zeros((1, 128), F32)
    inside_sum, mixed_sum = lax.fori_loop(0, blocks // 16, energies, (blank, blank))
    mine = jnp.where(row == 0, inside_sum, jnp.where(row == 1, mixed_sum, level))
    energy[2, here] = mine

    def energy_copy(kind, other, slot):
        line = above if kind == 0 else below if kind == 1 else {}
        return pltpu.make_async_remote_copy(
            src_ref=energy.at[2, here],
            dst_ref=energy.at[kind, slot],
            send_sem=energy_send.at[kind, other],
            recv_sem=energy_recv.at[kind, slot],
            device_id=mate_slab(line, other),
            device_id_type=MESH,
        )

    def send_energy(kind, start):
        for other in range(start, n_slab):
            energy_copy(kind, other, here).start()

    def receive_energy(kind, start):
        for other in range(start, n_slab):
            energy_copy(kind, other, lax.rem(here + other, n_slab)).wait_recv()

    def sent_energy(kind, start):
        for other in range(start, n_slab):
            energy_copy(kind, other, here).wait_send()

    pl.when(has_above)(lambda: send_energy(0, 0))
    pl.when(has_below)(lambda: send_energy(1, 0))
    send_energy(2, 1)

    mate = partner[0]
    taken = accept[0] == 1
    from_below = jnp.full((8, 128), jnp.where(taken & (mate == rep - 1), 1, 0)) == 1
    from_above = jnp.full((8, 128), jnp.where(taken & (mate == rep + 1), 1, 0)) == 1
    wait_pair(state_copy)
    for kind, result in ((0, new_pos), (1, new_vel)):

        def choose(t, carry):
            at = pl.ds(pl.multiple_of(t * 8, 8), 8)
            held = pl.ds(pl.multiple_of(3 * kind * blocks + t * 8, 8), 8)
            value = jnp.where(from_below, swapped[0, held, :], state[held, :])
            result[at, :] = jnp.where(from_above, swapped[1, held, :], value)
            return carry

        lax.fori_loop(0, 3 * blocks // 8, choose, 0)

    leaves = [
        pltpu.make_async_copy(new_pos, new_pos_far, leave.at[0]),
        pltpu.make_async_copy(new_vel, new_vel_far, leave.at[1]),
    ]
    for copy in leaves:
        copy.start()

    pl.when(has_above)(lambda: sent_energy(0, 0))
    pl.when(has_below)(lambda: sent_energy(1, 0))
    sent_energy(2, 1)
    receive_energy(2, 1)
    pl.when(has_below)(lambda: receive_energy(0, 0))
    pl.when(has_above)(lambda: receive_energy(1, 0))

    def whole(kind):
        every = energy[kind, 0]
        for slot in range(1, n_slab):
            every = every + energy[kind, slot]
        every = 0.5 * jnp.sum(every, axis=1, keepdims=True)
        return jnp.where(row == 2, energy[kind, 0], jnp.broadcast_to(every, (8, 128)))

    every = whole(2)
    is_below = jnp.full((8, 128), jnp.where(mate == rep - 1, 1, 0)) == 1
    is_above = jnp.full((8, 128), jnp.where(mate == rep + 1, 1, 0)) == 1
    theirs = jnp.where(is_below, whole(0), jnp.where(is_above, whole(1), every))
    gap = every - theirs
    far_level = theirs[2:3]
    near_level = every[2:3]
    answer = (far_level - near_level) * gap[0:1] + (
        jnp.sqrt(far_level) - jnp.sqrt(near_level)
    ) * gap[1:2]
    answer = answer / F32(total * 128)
    exponent[...] = jnp.broadcast_to(answer, (8, 128))
    for copy in leaves:
        copy.wait()


def hand_over(pos, vel, tile, new_pos, new_vel, exponent):
    new_pos[...] = pos[...]
    new_vel[...] = vel[...]
    exponent[...] = tile[0:1, 0:1]


def shards(
    positions, velocities, strength, inv_mass, solute, scales, neighbours, counts, partner, accept
):
    n_rep = lax.axis_size("rep")
    n_slab = lax.axis_size("slab")
    atoms = positions.shape[2]
    blocks = atoms // 128
    wide = blocks + 2 * RIM
    pairs = 3 * blocks * NB * 128 * 128
    smem = pl.BlockSpec(memory_space=pltpu.SMEM)
    vmem = pl.BlockSpec(memory_space=pltpu.VMEM)
    far = pl.BlockSpec(memory_space=pltpu.HBM)
    rowed = (blocks, 128)
    new_pos, new_vel, exponent = pl.pallas_call(
        functools.partial(kernel, n_rep, n_slab, blocks),
        out_shape=(
            jax.ShapeDtypeStruct((3 * blocks, 128), F32),
            jax.ShapeDtypeStruct((3 * blocks, 128), F32),
            jax.ShapeDtypeStruct((8, 128), F32),
        ),
        in_specs=[pl.BlockSpec(memory_space=pltpu.HBM)] * 10,
        out_specs=(far, far, vmem),
        scratch_shapes=[
            pltpu.VMEM((3 * blocks, 128), F32),
            pltpu.VMEM((3 * blocks, 128), F32),
            pltpu.SemaphoreType.DMA((2,)),
            pltpu.SMEM((1,), F32),
            pltpu.SMEM((NB, blocks), jnp.int32),
            pltpu.SMEM((blocks,), jnp.int32),
            pltpu.SMEM((1,), jnp.int32),
            pltpu.SMEM((1,), jnp.int32),
            pltpu.VMEM((3 * blocks, 128), F32),
            pltpu.VMEM((3 * blocks, 128), F32),
            pltpu.VMEM(rowed, F32),
            pltpu.VMEM(rowed, F32),
            pltpu.VMEM(rowed, jnp.int32),
            pltpu.SemaphoreType.DMA((10,)),
            pltpu.SMEM((blocks * NB,), jnp.int32),
            pltpu.VMEM((blocks, 8, 128), F32),
            pltpu.VMEM((blocks, 8, 128), F32),
            pltpu.VMEM((blocks, 8, 128), F32),
            pltpu.VMEM((blocks, 48, 128), BF16),
            pltpu.VMEM((wide + 1, 48, 128), BF16),
            pltpu.VMEM((wide + 1, 16, 128), BF16),
            pltpu.VMEM((blocks, 8, 128), F32),
            pltpu.VMEM((4, blocks, 128), F32),
            pltpu.VMEM((3, 2, RIM, 4, 128), F32),
            pltpu.VMEM((3, 2, RIM, 4, 128), F32),
            pltpu.VMEM((6 * blocks, 128), F32),
            pltpu.VMEM((2, 6 * blocks, 128), F32),
            pltpu.VMEM((3, n_slab, 8, 128), F32),
            pltpu.SemaphoreType.DMA((3, 2)),
            pltpu.SemaphoreType.DMA((3, 2)),
            pltpu.SemaphoreType.DMA((2,)),
            pltpu.SemaphoreType.DMA((2,)),
            pltpu.SemaphoreType.DMA((3, n_slab)),
            pltpu.SemaphoreType.DMA((3, n_slab)),
        ],
        compiler_params=pltpu.CompilerParams(
            collective_id=0, has_side_effects=True, vmem_limit_bytes=56 << 20
        ),
        cost_estimate=pl.CostEstimate(
            flops=pairs * 100, bytes_accessed=1 << 20, transcendentals=pairs
        ),
    )(
        scales,
        neighbours.T,
        counts,
        partner,
        accept,
        positions.reshape(3 * blocks, 128),
        velocities.reshape(3 * blocks, 128),
        strength.reshape(rowed),
        inv_mass.reshape(rowed),
        solute.reshape(rowed),
    )
    shape = positions.shape
    new_pos, new_vel, exponent = pl.pallas_call(
        hand_over,
        out_shape=(
            jax.ShapeDtypeStruct((3 * blocks, 128), F32),
            jax.ShapeDtypeStruct((3 * blocks, 128), F32),
            jax.ShapeDtypeStruct((1, 1), F32),
        ),
        in_specs=[vmem, vmem, vmem],
        out_specs=(vmem, vmem, vmem),
    )(new_pos, new_vel, exponent)
    return (new_pos.reshape(shape), new_vel.reshape(shape), exponent.reshape(1))


def solution(mesh):
    placed = (
        P("rep", None, "slab"),
        P("rep", None, "slab"),
        P("slab"),
        P("slab"),
        P("slab"),
        P("rep"),
        P("slab", None),
        P("slab"),
        P("rep"),
        P("rep"),
    )
    return jax.shard_map(
        shards,
        mesh=mesh,
        in_specs=placed,
        out_specs=(P("rep", None, "slab"), P("rep", None, "slab"), P("rep")),
        check_vma=False,
    )
```

```python
import functools
import math

import jax
import jax.numpy as jnp
from jax import lax
from jax.experimental import pallas as pl
from jax.experimental.pallas import tpu as pltpu
from jax.sharding import PartitionSpec as P

NB = 4
RIM = 16
SIGMA = 0.35
BOX = 2.0
STEP = 0.02
NONE = -1000.0
MESH = pl.DeviceIdType.MESH
F32 = jnp.float32
BF16 = jnp.bfloat16
SINE = (
    6.28318530717,
    -41.34170211,
    81.60522621,
    -76.70428132,
    42.00980576,
    -14.39413556,
)


def dot(a, b):
    return jnp.dot(a, b, preferred_element_type=F32)


def dot_left(a, b):
    return lax.dot_general(a, b, (((0,), (0,)), ((), ())), preferred_element_type=F32)


def parts(value):
    first = value.astype(BF16).astype(F32)
    rest = value - first
    second = rest.astype(BF16).astype(F32)
    third = rest - second
    return first, second, third


def kernel(
    n_rep,
    n_slab,
    blocks,
    scales_far,
    listed_far,
    counts_far,
    partner_far,
    accept_far,
    positions_far,
    velocities_far,
    strength_far,
    inv_mass_far,
    solute_far,
    new_pos,
    new_vel,
    exponent,
    scales,
    listed,
    counts,
    partner,
    accept,
    positions,
    velocities,
    strength,
    inv_mass,
    solute,
    fetch,
    pick,
    pos8,
    vel8,
    feat8,
    own,
    far,
    flagged,
    acc,
    rows,
    stage,
    halo,
    state,
    swapped,
    energy,
    halo_send,
    halo_recv,
    state_send,
    state_recv,
    energy_send,
    energy_recv,
):
    rep = lax.axis_index("rep")
    here = lax.axis_index("slab")
    above = {"rep": jnp.minimum(rep + 1, n_rep - 1)}
    below = {"rep": jnp.maximum(rep - 1, 0)}
    after = {"slab": lax.rem(here + 1, n_slab)}
    before = {"slab": lax.rem(here + n_slab - 1, n_slab)}
    wide = blocks + 2 * RIM

    fetches = [
        pltpu.make_async_copy(source, target, fetch.at[i])
        for i, (source, target) in enumerate(
            (
                (strength_far, strength),
                (solute_far, solute),
                (inv_mass_far, inv_mass),
                (scales_far, scales),
                (positions_far, positions),
                (velocities_far, velocities),
                (listed_far, listed),
                (counts_far, counts),
                (partner_far, partner),
                (accept_far, accept),
            )
        )
    ]
    for copy in fetches:
        copy.start()
    barrier = pltpu.get_barrier_semaphore()
    has_below = rep > 0
    has_above = rep < n_rep - 1

    def mate_slab(line, other):
        return {**line, "slab": lax.rem(here + other, n_slab)}

    def greet(line, start):
        for other in range(start, n_slab):
            pl.semaphore_signal(
                barrier, 1, device_id=mate_slab(line, other), device_id_type=MESH
            )

    pl.when(has_above)(lambda: greet(above, 0))
    greet({}, 1)
    pl.when(has_below)(lambda: greet(below, 0))

    row = lax.broadcasted_iota(jnp.int32, (8, 128), 0)
    long = (row == 0) | (row == 4)
    is3 = row == 3
    is7 = row == 7
    periods = (float(n_slab), BOX)
    inverse = jnp.where(long, F32(1.0 / periods[0]), F32(1.0 / periods[1]))
    phase = jnp.where(row >= 4, F32(0.25), F32(0.0))
    heights = [p * p / (2.0 * math.pi**2) / (2.0 * SIGMA**2) for p in periods]
    height = jnp.where(long, F32(math.sqrt(heights[0])), F32(math.sqrt(heights[1])))
    shift = heights[0] + 2.0 * heights[1]
    slope = [STEP * p / math.pi / (2.0 * SIGMA**2) / h for p, h in zip(periods, heights)]
    slope = jnp.where(long, F32(slope[0]), F32(slope[1]))
    slope = jnp.where(is3 | is7, F32(0.0), jnp.where(row >= 4, -slope, slope))

    def features(x):
        turn = x * inverse - phase
        turn = turn - jnp.floor(turn + 0.5)
        w = 0.25 - jnp.abs(turn)
        z = w * w
        value = F32(SINE[-1])
        for c in SINE[-2::-1]:
            value = value * z + F32(c)
        return value * (w * height)

    fixed = parts(jnp.where(is3, F32(-shift), F32(1.0)))

    def put(spot, value, log_weight, owned):
        value = jnp.where(is3, F32(1.0), jnp.where(is7, log_weight, value))
        a, b, c = parts(value)
        far[spot] = jnp.concatenate([a, b, c, a, b, a], axis=0).astype(BF16)
        if owned:
            x, y, z = [jnp.where(is3 | is7, k, v) for k, v in zip(fixed, (a, b, c))]
            own[spot] = jnp.concatenate([x, x, x, y, y, z], axis=0).astype(BF16)

    for copy in fetches:
        copy.wait()

    level = jnp.full((8, 128), scales[0], F32)
    root = jnp.sqrt(level)

    def atom_rows(t, carry):
        at = pl.ds(pl.multiple_of(t * 8, 8), 8)
        plain = strength[at, :]
        chosen = solute[at, :] == 1
        scaled = plain * jnp.where(chosen, root, F32(1.0))
        rows[0, at, :] = jnp.log(scaled)
        rows[1, at, :] = jnp.log(plain)
        rows[2, at, :] = jnp.where(chosen, F32(1.0), F32(0.0))
        rows[3, at, :] = scaled * inv_mass[at, :]
        return carry

    lax.fori_loop(0, blocks // 8, atom_rows, 0)

    def one_row(which, b):
        return rows[which, pl.ds(b, 1), :]

    def put_stage(turn, side, i, x, extra):
        stage[turn, side, i] = jnp.where(is3, extra, x)[:4]

    def load(b):
        blank = jnp.zeros((1, 128), F32)
        x = positions[pl.ds(b, 3, stride=blocks), :]
        v = velocities[pl.ds(b, 3, stride=blocks), :]
        pos8[b] = jnp.concatenate([x, blank, x, blank], axis=0)
        vel8[b] = jnp.concatenate([v, blank, v, blank], axis=0)

    def load_some(t, carry):
        for u in range(4):
            load(t * 4 + u)
        return carry

    lax.fori_loop(0, blocks // 4, load_some, 0)

    def stage_first(i, carry):
        low = i
        high = blocks - RIM + i
        put_stage(0, 0, i, pos8[low], one_row(0, low))
        put_stage(0, 1, i, pos8[high], one_row(0, high))
        return carry

    lax.fori_loop(0, RIM, stage_first, 0)
    lines = has_below.astype(jnp.int32) + has_above.astype(jnp.int32)
    pl.semaphore_wait(barrier, n_slab - 1 + n_slab * lines)

    def halo_copy(turn, side):
        return pltpu.make_async_remote_copy(
            src_ref=stage.at[turn, side],
            dst_ref=halo.at[turn, side],
            send_sem=halo_send.at[turn, side],
            recv_sem=halo_recv.at[turn, side],
            device_id=before if side == 0 else after,
            device_id_type=MESH,
        )

    def send_halo(turn):
        for side in range(2):
            halo_copy(turn, side).start()

    send_halo(0)

    first = here * blocks
    total = n_slab * blocks

    def find(b, carry):
        count = counts[b]
        for k in range(1, NB):
            near = listed[k, b] - first
            near = jnp.where(near < 0, near + total, near)
            near = jnp.where(near < blocks + RIM, near, near - (total - blocks - 2 * RIM))
            pick[b * NB + k] = jnp.where(k < count, near, wide)
        return carry

    lax.fori_loop(0, blocks, find, 0)

    far[wide] = jnp.concatenate(
        [jnp.where(is7, F32(NONE), F32(0.0)), jnp.zeros((40, 128), F32)], axis=0
    ).astype(BF16)

    def own_features(which):
        def some(t, carry):
            for u in range(12):
                b = t * 12 + u
                value = features(pos8[b])
                feat8[b] = value
                put(b, value, one_row(which, b), True)
            return carry

        lax.fori_loop(0, blocks // 12, some, 0)

    def halo_features(turn):
        log_turn = 1 if turn == 2 else 0

        def some(t, carry):
            for side in range(2):
                for u in range(4):
                    i = t * 4 + u
                    got = halo[turn, side, i]
                    value = features(jnp.concatenate([got, got], axis=0))
                    put(blocks + side * RIM + i, value, halo[log_turn, side, i][3:4], False)
                    if turn == 2:
                        put_flags(blocks + side * RIM + i, got[3:4])
            return carry

        lax.fori_loop(0, RIM // 4, some, 0)

    def put_flags(spot, flags):
        flagged[spot] = jnp.where(
            lax.broadcasted_iota(jnp.int32, (16, 128), 0) == 0, flags, F32(1.0)
        ).astype(BF16)

    def exponents(picks, b):
        ahead = jnp.concatenate([far[n] for n in picks], axis=1)
        return dot_left(ahead, own[b])

    def sums(columns, picks, b, exps):
        values = jnp.exp(exps)
        weights = jnp.concatenate([columns(n) for n in picks], axis=1)
        high = values.astype(BF16)
        low = (values - high.astype(F32)).astype(BF16)
        return dot(weights, high) + dot(weights, low)

    def all_sums(one, picked):
        exps = [exponents(picks, b) for picks, b in picked]
        return [one(picks, b, y) for (picks, b), y in zip(picked, exps)]

    def force_columns(n):
        return far[n, :32, :]

    def force_sums(picks, b, exps):
        found = sums(force_columns, picks, b, exps)
        return found[0:8] + found[8:16] + found[16:24]

    def self_pass(amount, one):
        def some(t, carry):
            found = all_sums(one, [([t * amount + u], t * amount + u) for u in range(amount)])
            for u in range(amount):
                acc[t * amount + u] = found[u]
            return carry

        lax.fori_loop(0, blocks // amount, some, 0)

    def move(b, found):
        value = feat8[b]
        found = found * pltpu.roll(value, 4, 0)
        found = found - pltpu.roll(found, 4, 0)
        vel = vel8[b] + slope * one_row(3, b) * found
        pos = pos8[b] + F32(STEP) * vel
        return pos, vel

    def picks_of(b):
        return [pick[b * NB + k] for k in range(1, NB)]

    def force_pass(turn):
        def rim(t, carry):
            spots = [t * 8 + u for u in range(8)] + [blocks - RIM + t * 8 + u for u in range(8)]
            found = all_sums(force_sums, [(picks_of(b), b) for b in spots])
            for u, b in enumerate(spots):
                pos, vel = move(b, found[u] + acc[b])
                keep(turn, b, pos, vel)
                put_stage(turn + 1, u // 8, t * 8 + u % 8, pos, one_row(1 + turn, b))
            return carry

        lax.fori_loop(0, RIM // 8, rim, 0)
        send_halo(turn + 1)

        def inner(t, carry):
            spots = [RIM + t * 16 + u for u in range(16)]
            found = all_sums(force_sums, [(picks_of(b), b) for b in spots])
            for u, b in enumerate(spots):
                pos, vel = move(b, found[u] + acc[b])
                keep(turn, b, pos, vel)
            return carry

        lax.fori_loop(0, (blocks - 2 * RIM) // 16, inner, 0)

    def keep(turn, b, pos, vel):
        pos8[b] = pos
        if turn == 0:
            vel8[b] = vel
        else:
            state[pl.ds(b, 3, stride=blocks), :] = pos[:3]
            state[pl.ds(3 * blocks + b, 3, stride=blocks), :] = vel[:3]

    def state_copy(side):
        return pltpu.make_async_remote_copy(
            src_ref=state,
            dst_ref=swapped.at[side],
            send_sem=state_send.at[side],
            recv_sem=state_recv.at[side],
            device_id=above if side == 0 else below,
            device_id_type=MESH,
        )

    def finish_halo(turn):
        for side in range(2):
            halo_copy(turn, side).wait()

    for turn in range(2):
        own_features(0)
        self_pass(24, force_sums)
        finish_halo(turn)
        halo_features(turn)
        force_pass(turn)

    def start_pair(copy):
        pl.when(has_above)(lambda: copy(0).start())
        pl.when(has_below)(lambda: copy(1).start())

    def wait_pair(copy):
        @pl.when(has_above)
        def _():
            copy(0).wait_send()
            copy(1).wait_recv()

        @pl.when(has_below)
        def _():
            copy(1).wait_send()
            copy(0).wait_recv()

    start_pair(state_copy)

    own_features(1)

    def own_flags(b, carry):
        put_flags(b, one_row(2, b))
        return carry

    lax.fori_loop(0, blocks, own_flags, 0)
    flagged[wide] = jnp.zeros((16, 128), BF16)

    def energy_columns(n):
        return flagged[n]

    def energy_sums(picks, b, exps):
        return sums(energy_columns, picks, b, exps)[:8]

    self_pass(24, energy_sums)
    finish_halo(2)
    halo_features(2)

    def energies(t, carry):
        spots = [t * 16 + u for u in range(16)]
        found = all_sums(energy_sums, [(picks_of(b), b) for b in spots])
        inside_sum, mixed_sum = carry
        for u, b in enumerate(spots):
            both = found[u] + acc[b]
            inside = both[0:1]
            every = both[1:2]
            flags = one_row(2, b)
            plain = strength[pl.ds(b, 1), :]
            inside_sum = inside_sum + plain * flags * inside
            mixed_sum = mixed_sum + plain * (
                flags * (every - inside) + (F32(1.0) - flags) * inside
            )
        return inside_sum, mixed_sum

    blank = jnp.zeros((1, 128), F32)
    inside_sum, mixed_sum = lax.fori_loop(0, blocks // 16, energies, (blank, blank))
    mine = jnp.where(row == 0, inside_sum, jnp.where(row == 1, mixed_sum, level))
    energy[2, here] = mine

    def energy_copy(kind, other, slot):
        line = above if kind == 0 else below if kind == 1 else {}
        return pltpu.make_async_remote_copy(
            src_ref=energy.at[2, here],
            dst_ref=energy.at[kind, slot],
            send_sem=energy_send.at[kind, other],
            recv_sem=energy_recv.at[kind, slot],
            device_id=mate_slab(line, other),
            device_id_type=MESH,
        )

    def send_energy(kind, start):
        for other in range(start, n_slab):
            energy_copy(kind, other, here).start()

    def receive_energy(kind, start):
        for other in range(start, n_slab):
            energy_copy(kind, other, lax.rem(here + other, n_slab)).wait_recv()

    def sent_energy(kind, start):
        for other in range(start, n_slab):
            energy_copy(kind, other, here).wait_send()

    pl.when(has_above)(lambda: send_energy(0, 0))
    pl.when(has_below)(lambda: send_energy(1, 0))
    send_energy(2, 1)

    mate = partner[0]
    taken = accept[0] == 1
    from_below = jnp.full((8, 128), jnp.where(taken & (mate == rep - 1), 1, 0)) == 1
    from_above = jnp.full((8, 128), jnp.where(taken & (mate == rep + 1), 1, 0)) == 1
    wait_pair(state_copy)
    for kind, result in ((0, new_pos), (1, new_vel)):

        def choose(t, carry):
            at = pl.ds(pl.multiple_of(t * 8, 8), 8)
            held = pl.ds(pl.multiple_of(3 * kind * blocks + t * 8, 8), 8)
            value = jnp.where(from_below, swapped[0, held, :], state[held, :])
            result[at, :] = jnp.where(from_above, swapped[1, held, :], value)
            return carry

        lax.fori_loop(0, 3 * blocks // 8, choose, 0)

    pl.when(has_above)(lambda: sent_energy(0, 0))
    pl.when(has_below)(lambda: sent_energy(1, 0))
    sent_energy(2, 1)
    receive_energy(2, 1)
    pl.when(has_below)(lambda: receive_energy(0, 0))
    pl.when(has_above)(lambda: receive_energy(1, 0))

    def whole(kind):
        every = energy[kind, 0]
        for slot in range(1, n_slab):
            every = every + energy[kind, slot]
        every = 0.5 * jnp.sum(every, axis=1, keepdims=True)
        return jnp.where(row == 2, energy[kind, 0], jnp.broadcast_to(every, (8, 128)))

    every = whole(2)
    is_below = jnp.full((8, 128), jnp.where(mate == rep - 1, 1, 0)) == 1
    is_above = jnp.full((8, 128), jnp.where(mate == rep + 1, 1, 0)) == 1
    theirs = jnp.where(is_below, whole(0), jnp.where(is_above, whole(1), every))
    gap = every - theirs
    far_level = theirs[2:3]
    near_level = every[2:3]
    answer = (far_level - near_level) * gap[0:1] + (
        jnp.sqrt(far_level) - jnp.sqrt(near_level)
    ) * gap[1:2]
    answer = answer / F32(total * 128)
    exponent[...] = jnp.broadcast_to(answer, (8, 128))


def hand_over(pos, vel, tile, new_pos, new_vel, exponent):
    new_pos[...] = pos[...]
    new_vel[...] = vel[...]
    exponent[...] = tile[0:1, 0:1]


def shards(
    positions, velocities, strength, inv_mass, solute, scales, neighbours, counts, partner, accept
):
    n_rep = lax.axis_size("rep")
    n_slab = lax.axis_size("slab")
    atoms = positions.shape[2]
    blocks = atoms // 128
    wide = blocks + 2 * RIM
    pairs = 3 * blocks * NB * 128 * 128
    smem = pl.BlockSpec(memory_space=pltpu.SMEM)
    vmem = pl.BlockSpec(memory_space=pltpu.VMEM)
    far = pl.BlockSpec(memory_space=pltpu.HBM)
    rowed = (blocks, 128)
    new_pos, new_vel, exponent = pl.pallas_call(
        functools.partial(kernel, n_rep, n_slab, blocks),
        out_shape=(
            jax.ShapeDtypeStruct((3 * blocks, 128), F32),
            jax.ShapeDtypeStruct((3 * blocks, 128), F32),
            jax.ShapeDtypeStruct((8, 128), F32),
        ),
        in_specs=[pl.BlockSpec(memory_space=pltpu.HBM)] * 10,
        out_specs=(vmem, vmem, vmem),
        scratch_shapes=[
            pltpu.SMEM((1,), F32),
            pltpu.SMEM((NB, blocks), jnp.int32),
            pltpu.SMEM((blocks,), jnp.int32),
            pltpu.SMEM((1,), jnp.int32),
            pltpu.SMEM((1,), jnp.int32),
            pltpu.VMEM((3 * blocks, 128), F32),
            pltpu.VMEM((3 * blocks, 128), F32),
            pltpu.VMEM(rowed, F32),
            pltpu.VMEM(rowed, F32),
            pltpu.VMEM(rowed, jnp.int32),
            pltpu.SemaphoreType.DMA((10,)),
            pltpu.SMEM((blocks * NB,), jnp.int32),
            pltpu.VMEM((blocks, 8, 128), F32),
            pltpu.VMEM((blocks, 8, 128), F32),
            pltpu.VMEM((blocks, 8, 128), F32),
            pltpu.VMEM((blocks, 48, 128), BF16),
            pltpu.VMEM((wide + 1, 48, 128), BF16),
            pltpu.VMEM((wide + 1, 16, 128), BF16),
            pltpu.VMEM((blocks, 8, 128), F32),
            pltpu.VMEM((4, blocks, 128), F32),
            pltpu.VMEM((3, 2, RIM, 4, 128), F32),
            pltpu.VMEM((3, 2, RIM, 4, 128), F32),
            pltpu.VMEM((6 * blocks, 128), F32),
            pltpu.VMEM((2, 6 * blocks, 128), F32),
            pltpu.VMEM((3, n_slab, 8, 128), F32),
            pltpu.SemaphoreType.DMA((3, 2)),
            pltpu.SemaphoreType.DMA((3, 2)),
            pltpu.SemaphoreType.DMA((2,)),
            pltpu.SemaphoreType.DMA((2,)),
            pltpu.SemaphoreType.DMA((3, n_slab)),
            pltpu.SemaphoreType.DMA((3, n_slab)),
        ],
        compiler_params=pltpu.CompilerParams(
            collective_id=0, has_side_effects=True, vmem_limit_bytes=56 << 20
        ),
        cost_estimate=pl.CostEstimate(
            flops=pairs * 100, bytes_accessed=1 << 20, transcendentals=pairs
        ),
    )(
        scales,
        neighbours.T,
        counts,
        partner,
        accept,
        positions.reshape(3 * blocks, 128),
        velocities.reshape(3 * blocks, 128),
        strength.reshape(rowed),
        inv_mass.reshape(rowed),
        solute.reshape(rowed),
    )
    shape = positions.shape
    new_pos, new_vel, exponent = pl.pallas_call(
        hand_over,
        out_shape=(
            jax.ShapeDtypeStruct((3 * blocks, 128), F32),
            jax.ShapeDtypeStruct((3 * blocks, 128), F32),
            jax.ShapeDtypeStruct((1, 1), F32),
        ),
        in_specs=[vmem, vmem, vmem],
        out_specs=(vmem, vmem, vmem),
    )(new_pos, new_vel, exponent)
    return (new_pos.reshape(shape), new_vel.reshape(shape), exponent.reshape(1))


def solution(mesh):
    placed = (
        P("rep", None, "slab"),
        P("rep", None, "slab"),
        P("slab"),
        P("slab"),
        P("slab"),
        P("rep"),
        P("slab", None),
        P("slab"),
        P("rep"),
        P("rep"),
    )
    return jax.shard_map(
        shards,
        mesh=mesh,
        in_specs=placed,
        out_specs=(P("rep", None, "slab"), P("rep", None, "slab"), P("rep")),
        check_vma=False,
    )
```
